256 devices in a mesh: inst: 32 (over x, z_lo, core), tp: 8 (over z_hi, y).
Axes of the slice: x: 4, y: 4, z: 8 (z_hi: 2, z_lo: 4; z = z_hi * 4 + z_lo), core: 2. Of those that a mesh axis runs over, the one named last changes fastest.
Arguments:
- keys_cache: bfloat16 [32, 4, 1024, 8, 128], P('inst', None, None, 'tp'), may hold values from -4 to 4
- values_cache: bfloat16 [32, 4, 1024, 8, 128], P('inst', None, None, 'tp'), may hold values from -4 to 4
- queries: bfloat16 [4, 64, 8192], P(None, 'inst', 'tp'), may hold values from -9 to 9
- fresh_keys: bfloat16 [4, 64, 1024], P(None, 'inst', 'tp'), may hold values from -6 to 6
- fresh_values: bfloat16 [4, 64, 1024], P(None, 'inst', 'tp'), may hold values from -6 to 6
- out_weight: bfloat16 [8192, 4096], P('tp'), may hold values from -0.5 to 0.5
- partner: int32 [16], replicated, may hold values from 0 to 15, each once
- chosen: int32 [16, 4], replicated, may hold values from 0 to 1, as said below
- lengths: int32 [16, 4], replicated, may hold values from 2 to 2048, as said below
- dest_slot: int32 [16, 4], replicated, may hold values from 0 to 3, each once within a row
Outputs:
- moved_keys: bfloat16 [32, 4, 1024, 8, 128], P('inst', None, None, 'tp')
- moved_values: bfloat16 [32, 4, 1024, 8, 128], P('inst', None, None, 'tp')
- mixed: bfloat16 [4, 64, 4096], P(None, 'inst', 'tp')
The draws below stay inside these ranges and needn't reach their ends.
Inputs may be any that keep to these rules, and one draw needn't show every extreme that they name: `partner`: a permutation of the 16 instances. `chosen`: each instance hands over one or two requests; in every draw some instance hands over exactly 2. `lengths`: in every instance some request has exactly 2048 positions. `dest_slot`: each row is a permutation of the 4 slots.
All inputs are finite; a program needn't handle non-finite values.
Results may differ from the reference program's by a relative error of at most 0.0056.
Values may be sent and summed in bfloat16 or wider, within the bound.
A program may use at most 64 MiB of HBM per device.

```python
import jax
import jax.numpy as jnp
from jax import lax

HQ = 64
KVH = 8
HD = 128
DOUT = 4096
ROWS = 4
CTX_DEV = 1024
NEW = 4
GROUP = 8
MOST = 2
INSTANCES = 16
HOLDERS = 32
TOKENS = 64
CTX = 2048


def draw_keys_cache(key, part):
    key = jax.random.fold_in(key, 1)
    shaped = (HOLDERS, ROWS, CTX_DEV, KVH, HD)
    return jnp.clip(jax.random.normal(key, shaped, jnp.float32), -4.0, 4.0).astype(jnp.bfloat16)


def draw_queries(key, part):
    key = jax.random.fold_in(key, 2)
    shaped = (NEW, TOKENS, HQ * HD)
    return jnp.clip(jax.random.normal(key, shaped, jnp.float32), -4.0, 4.0).astype(jnp.bfloat16)


def draw_chosen(key, part):
    key = jax.random.fold_in(key, 3)
    first_key, second_key, third_key = jax.random.split(key, 3)
    counts = jax.random.randint(first_key, (INSTANCES,), max(1, MOST // 2), MOST + 1)
    fullest = jax.random.randint(second_key, (), 0, INSTANCES)
    counts = jnp.where(jnp.arange(INSTANCES) == fullest, MOST, counts)
    orders = jax.vmap(lambda single: jax.random.permutation(single, ROWS))(jax.random.split(third_key, INSTANCES))
    ranks = jnp.argsort(orders, axis=1, stable=True)
    return (ranks < counts[:, None]).astype(jnp.int32)


def draw_lengths(key, part):
    key = jax.random.fold_in(key, 4)
    first_key, second_key = jax.random.split(key, 2)
    spans = jax.random.randint(first_key, (INSTANCES, ROWS), 2, CTX + 1)
    longest = jax.random.randint(second_key, (INSTANCES,), 0, ROWS)
    return jnp.where(jnp.arange(ROWS)[None, :] == longest[:, None], CTX, spans).astype(jnp.int32)


def levels(stream_key, dims, pieces, least, largest):
    def one(axis_at, shards_of):
        draws = jax.random.uniform(jax.random.fold_in(jax.random.fold_in(stream_key, 6), axis_at), (shards_of,), jnp.float32, least / len(pieces), largest / len(pieces))
        return jnp.repeat(jnp.exp(draws), dims[axis_at] // shards_of).reshape((-1,) + (1,) * (len(dims) - axis_at - 1))

    loudness = one(*pieces[0])
    for cut in pieces[1:]:
        loudness = loudness * one(*cut)
    return loudness


def centred(rng, dims, deviation, reach, pieces=(), kind=jnp.bfloat16):
    drawn = deviation * jax.random.normal(rng, dims, jnp.float32)
    if pieces:
        drawn = drawn * levels(rng, dims, pieces, -0.22, 0.18)
    return jnp.clip(drawn, -reach, reach).astype(kind)


def setup_inputs(seed: int = 0) -> dict:
    keys = jax.random.split(jax.random.key(seed), 11)
    keys_cache = draw_keys_cache(jax.random.fold_in(keys[10], 71), 0)
    values_cache = centred(keys[1], (HOLDERS, ROWS, CTX_DEV, KVH, HD), 1.0, 4.0, ((0, 32), (3, 8)))
    queries = draw_queries(jax.random.fold_in(keys[10], 71), 0)
    fresh_keys = centred(keys[3], (NEW, TOKENS, KVH * HD), 1.0, 6.0, ((1, 32), (2, 8)))
    fresh_values = centred(keys[4], (NEW, TOKENS, KVH * HD), 1.0, 6.0, ((1, 32), (2, 8)))
    out_weight = centred(keys[5], (HQ * HD, DOUT), HD ** -0.5, 0.5, ((0, 8),))
    partner = jax.random.permutation(keys[6], INSTANCES).astype(jnp.int32)
    chosen = draw_chosen(jax.random.fold_in(keys[10], 71), 0)
    lengths = draw_lengths(jax.random.fold_in(keys[10], 71), 0)
    dest_slot = jax.vmap(lambda own: jax.random.permutation(own, ROWS))(jax.random.split(keys[9], INSTANCES)).reshape((INSTANCES, ROWS)).astype(jnp.int32)
    return {"keys_cache": keys_cache, "values_cache": values_cache, "queries": queries, "fresh_keys": fresh_keys, "fresh_values": fresh_values, "out_weight": out_weight, "partner": partner, "chosen": chosen, "lengths": lengths, "dest_slot": dest_slot}


big_negative = -1e30


def half_partial(block_keys, block_values, asking, span_len, offset):
    scaling = block_keys.shape[3] ** -0.5
    scores = jnp.einsum("rkqd,rpkd->rkqp", asking.astype(jnp.float32), block_keys.astype(jnp.float32)) * scaling
    places = offset + jnp.arange(block_keys.shape[1], dtype=jnp.int32)
    usable = (places[None, :] < span_len[:, None])[:, None, None, :]
    highest = jnp.max(jnp.where(usable, scores, big_negative), axis=3)
    weights = jnp.where(usable, jnp.exp(scores - highest[..., None]), 0.0)
    totals = jnp.sum(weights, axis=3)
    rounded = lax.optimization_barrier(weights.astype(jnp.bfloat16)).astype(jnp.float32)
    summed = jnp.einsum("rkqp,rpkd->rkqd", rounded, block_values.astype(jnp.float32))
    return summed, highest, totals


def combine(first_half, second_half, asking, fresh_key, fresh_value, new_count):
    scaling = asking.shape[3] ** -0.5
    scores = jnp.einsum("rkqd,mrkd->rkqm", asking.astype(jnp.float32), fresh_key.astype(jnp.float32)) * scaling
    query_rows = asking.shape[2]
    group_size = query_rows // new_count
    causal = (jnp.arange(query_rows, dtype=jnp.int32) // group_size)[:, None] >= jnp.arange(new_count, dtype=jnp.int32)[None, :]
    highest_new = jnp.max(jnp.where(causal, scores, big_negative), axis=3)
    ceiling = jnp.maximum(jnp.maximum(first_half[1], second_half[1]), highest_new)
    scale_first = jnp.exp(first_half[1] - ceiling)
    scale_second = jnp.exp(second_half[1] - ceiling)
    weights = jnp.where(causal, jnp.exp(scores - ceiling[..., None]), 0.0)
    totals = first_half[2] * scale_first + second_half[2] * scale_second + jnp.sum(weights, axis=3)
    summed = first_half[0] * scale_first[..., None] + second_half[0] * scale_second[..., None]
    summed = summed + jnp.einsum("rkqm,mrkd->rkqd", weights, fresh_value.astype(jnp.float32), precision=lax.Precision.HIGHEST)
    head_out = (summed / totals[..., None]).astype(jnp.bfloat16)
    row_count = head_out.shape[0]
    kv_count = head_out.shape[1]
    head_out = head_out.reshape(row_count, kv_count, new_count, group_size, head_out.shape[3])
    return head_out.transpose(2, 0, 1, 3, 4).reshape(new_count, row_count, kv_count * group_size * asking.shape[3])


def reference(keys_cache, values_cache, queries, fresh_keys, fresh_values, out_weight, partner, chosen, lengths, dest_slot):
    inst_ids = jnp.arange(INSTANCES, dtype=jnp.int32)
    slot_ids = jnp.arange(ROWS, dtype=jnp.int32)
    source_of = jnp.sum(jnp.where(partner[None, :] == inst_ids[:, None], inst_ids[None, :], 0), axis=1).astype(jnp.int32)
    from_mask = jnp.take(chosen, source_of, axis=0)
    from_slot = jnp.take(dest_slot, source_of, axis=0)
    matches = (from_mask[:, :, None] == 1) & (from_slot[:, :, None] == slot_ids[None, None, :])
    arrived = jnp.any(matches, axis=1)
    from_row = jnp.sum(jnp.where(matches, slot_ids[None, :, None], 0), axis=1).astype(jnp.int32)
    from_len = jnp.take_along_axis(jnp.take(lengths, source_of, axis=0), from_row, axis=1)
    spans_all = jnp.where(arrived, from_len, lengths)

    def relocate(cache):
        blocks = cache.reshape(INSTANCES, 2, ROWS, CTX_DEV, KVH, HD)

        def per_dest(target):
            anchor = lax.dynamic_index_in_dim(blocks, source_of[target], 0, keepdims=False)
            incoming = jnp.take(anchor, from_row[target], axis=1)
            resident = lax.dynamic_index_in_dim(blocks, target, 0, keepdims=False)
            return jnp.where(arrived[target][None, :, None, None, None], incoming, resident)

        return lax.map(per_dest, inst_ids).reshape(cache.shape)

    moved_keys = relocate(keys_cache)
    moved_values = relocate(values_cache)
    key_blocks = moved_keys.reshape(INSTANCES, 2, ROWS, CTX_DEV, KVH, HD)
    value_blocks = moved_values.reshape(INSTANCES, 2, ROWS, CTX_DEV, KVH, HD)

    def attend(target):
        keys_here = lax.dynamic_index_in_dim(key_blocks, target, 0, keepdims=False)
        values_here = lax.dynamic_index_in_dim(value_blocks, target, 0, keepdims=False)
        asking = lax.dynamic_slice_in_dim(queries, target * ROWS, ROWS, 1)
        asking = asking.reshape(NEW, ROWS, KVH, GROUP, HD).transpose(1, 2, 0, 3, 4).reshape(ROWS, KVH, NEW * GROUP, HD)
        span_len = spans_all[target]
        first_half = half_partial(keys_here[0], values_here[0], asking, span_len, 0)
        second_half = half_partial(keys_here[1], values_here[1], asking, span_len, CTX_DEV)
        fresh_key = lax.dynamic_slice_in_dim(fresh_keys, target * ROWS, ROWS, 1).reshape(NEW, ROWS, KVH, HD)
        fresh_value = lax.dynamic_slice_in_dim(fresh_values, target * ROWS, ROWS, 1).reshape(NEW, ROWS, KVH, HD)
        return combine(first_half, second_half, asking, fresh_key, fresh_value, NEW)

    head_all = lax.map(attend, inst_ids)
    head_all = head_all.transpose(1, 0, 2, 3).reshape(NEW * TOKENS, HQ * HD)
    mixed = jnp.dot(head_all, out_weight, preferred_element_type=jnp.float32)
    mixed = mixed.reshape(NEW, TOKENS, DOUT).astype(jnp.bfloat16)
    return moved_keys, moved_values, mixed
```

```python
import functools

import jax
import jax.numpy as jnp
from jax import lax
from jax.experimental import pallas as pl
from jax.experimental.pallas import tpu as pltpu
from jax.sharding import PartitionSpec as P

MESH = pl.DeviceIdType.MESH
LOW = -1e30
SLOTS = 4
MOST = 2
SIDE = 4
ITEMS = SIDE * MOST
WIDEST = ITEMS * 2
CAPS = (16,)
GROUPS = 4
SKEW = 4
LATER = 4
UP, DOWN, OUT, SEL, SPAN, PICK, NONE, WHICH, TABLE = 0, 16, 32, 40, 44, 48, 50, 51, 64


def where_am_i():
    inst = lax.axis_index("inst")
    chip = inst // 2
    return inst % 2, chip, chip // SIDE, chip % SIDE


def plan_kernel(partner, chosen, lengths, dest, table, count, start):
    _, me, _, z = where_am_i()
    sent = []
    for i in range(16):
        count[i] = 0
    for s in range(16):
        sent.append(sum(chosen[r, s] for r in range(SLOTS)))
        cls = (s % SIDE) * SIDE + partner[s] % SIDE
        count[cls] = count[cls] + sent[s]
    n = [[count[a * SIDE + b] for b in range(SIDE)] for a in range(SIDE)]

    def flip(a, b, down):
        return n[3 - a][3 - b] if down else n[a][b]

    need = 0
    for down in (False, True):
        f = functools.partial(flip, down=down)
        need = functools.reduce(
            jnp.maximum,
            (
                need,
                f(0, 1) + f(0, 2) + f(0, 3),
                f(0, 2) + f(0, 3) + f(1, 2) + f(1, 3),
                f(0, 3) + f(1, 3) + f(2, 3),
            ),
        )
    which, cap = 0, CAPS[0]
    for i in range(1, len(CAPS)):
        which = jnp.where(need > CAPS[i - 1], i, which)
        cap = jnp.where(need > CAPS[i - 1], CAPS[i], cap)
    for down in (False, True):
        f = functools.partial(flip, down=down)
        places = {
            (0, 3): 0,
            (1, 3): f(0, 3),
            (1, 2): f(0, 3) + f(1, 3),
            (0, 2): cap - f(0, 2),
            (0, 1): f(0, 3),
            (2, 3): f(0, 3) + f(1, 3),
        }
        for (a, b), place in places.items():
            start[(3 - a) * SIDE + 3 - b if down else a * SIDE + b] = place
    for a in range(SIDE):
        start[a * SIDE + a] = 0
    for c in range(WIDEST):
        table[UP + c] = jnp.where(z == 0, 0, ITEMS + c)
        table[DOWN + c] = jnp.where(z == SIDE - 1, 0, ITEMS + cap + c)
    for i in range(OUT, TABLE):
        table[i] = 0
    source = 0
    for s in range(16):
        d = partner[s]
        source = jnp.where(d == me, s, source)
        zs, xs = s % SIDE, s // SIDE
        zd, xd = d % SIDE, d // SIDE
        base = start[zs * SIDE + zd]
        start[zs * SIDE + zd] = base + sent[s]
        for j in range(MOST):
            valid = j < sent[s]
            leaves = valid & (zs == z) & (zd != zs)
            place = jnp.where(zd > zs, UP, DOWN) + base + j
            table[jnp.where(leaves, place, NONE)] = xs * MOST + j
            lands = valid & (zd == z)
            kept = jnp.where(zs < z, ITEMS + base + j, ITEMS + cap + base + j)
            kept = jnp.where(zs == z, xs * MOST + j, kept)
            table[jnp.where(lands, OUT + xd * MOST + j, NONE)] = kept
    mine, theirs = 0, 0
    for r in range(SLOTS):
        table[SPAN + r] = lengths[r, me]
    for r in range(SLOTS):
        go = chosen[r, me] == 1
        table[jnp.where(go, PICK + mine, NONE)] = r
        mine = mine + jnp.where(go, 1, 0)
        come = chosen[r, source] == 1
        slot = dest[r, source]
        theirs = theirs + jnp.where(come, 1, 0)
        table[jnp.where(come, SEL + slot, NONE)] = theirs
        table[jnp.where(come, SPAN + slot, NONE)] = lengths[r, source]
    table[WHICH] = which


def main_kernel(
    cap,
    table,
    q_ref,
    fresh_ref,
    k_ref,
    v_ref,
    w_hbm,
    mk_ref,
    mv_ref,
    mix_ref,
    w_buf,
    q_peer,
    x_out,
    x_in,
    pool,
    up_out,
    up_in,
    down_out,
    down_in,
    y_out,
    y_in,
    acc,
    top,
    tot,
    p_out,
    p_in,
    head,
    lhs,
    s_out,
    s_in,
    w_sem,
    q_sem,
    x_send,
    x_recv,
    up_send,
    up_recv,
    down_send,
    down_recv,
    y_send,
    y_recv,
    p_sem,
    s_send,
    s_recv,
):
    groups = x_out.shape[0]
    rows = x_out.shape[4]
    ctx = k_ref.shape[1]
    span = ctx // groups
    tps = s_out.shape[0]
    cols = s_out.shape[2]
    units = groups * cap
    half, chip, x, z = where_am_i()
    inst = lax.axis_index("inst")
    tp = lax.axis_index("tp")
    peer = (inst + 1 - 2 * half, tp)

    def along_x(dx):
        return (((x + dx) % SIDE * SIDE + z) * 2 + half, tp)

    above = (inst + 2, tp)
    below = (inst - 2, tp)

    barrier = pltpu.get_barrier_semaphore()

    def greet(device):
        pl.semaphore_signal(barrier, inc=1, device_id=device, device_id_type=MESH)

    greet(peer)
    for dx in range(1, SIDE):
        greet(along_x(dx))
    for dt in range(1, tps):
        greet((inst, (tp + dt) % tps))

    @pl.when(z < SIDE - 1)
    def _():
        greet(above)

    @pl.when(z > 0)
    def _():
        greet(below)

    w_copy = pltpu.make_async_copy(w_hbm, w_buf, w_sem)
    w_copy.start()

    def stage(g, carry):
        for dx in range(SIDE):
            to = (x + dx) % SIDE
            at = pl.ds(pl.multiple_of((g * SIDE + to) * rows, rows), rows)
            for j in range(MOST):
                slot = table[PICK + j]
                for kv, ref in enumerate((k_ref, v_ref)):
                    piece = ref[slot, at, :]
                    if dx == 0:
                        pool[g, x * MOST + j, kv] = piece
                    else:
                        x_out[g, dx - 1, j, kv] = piece
        return carry

    lax.fori_loop(0, groups, stage, 0)
    peers = 1 + (SIDE - 1) + (tps - 1)
    pl.semaphore_wait(
        barrier, peers + jnp.where(z > 0, 1, 0) + jnp.where(z < SIDE - 1, 1, 0)
    )

    q_copy = pltpu.make_async_remote_copy(
        q_ref, q_peer, q_sem.at[0], q_sem.at[1], device_id=peer, device_id_type=MESH
    )
    q_copy.start()

    def x_copy(g, dx):
        return pltpu.make_async_remote_copy(
            x_out.at[g, dx - 1],
            x_in.at[g, dx - 1],
            x_send.at[g, dx - 1],
            x_recv.at[g, dx - 1],
            device_id=along_x(dx),
            device_id_type=MESH,
        )

    def y_copy(g, dx):
        return pltpu.make_async_remote_copy(
            y_out.at[g, dx - 1],
            y_in.at[g, dx - 1],
            y_send.at[g, dx - 1],
            y_recv.at[g, dx - 1],
            device_id=along_x(dx),
            device_id_type=MESH,
        )

    def up_copy(k):
        return pltpu.make_async_remote_copy(
            up_out.at[k],
            up_in.at[k],
            up_send.at[k],
            up_recv.at[k],
            device_id=above,
            device_id_type=MESH,
        )

    def down_copy(k):
        return pltpu.make_async_remote_copy(
            down_out.at[k],
            down_in.at[k],
            down_send.at[k],
            down_recv.at[k],
            device_id=below,
            device_id_type=MESH,
        )

    def x_start(g, carry):
        for dx in (1, 3, 2):
            x_copy(g, dx).start()
        return carry

    lax.fori_loop(0, groups, x_start, 0)
    q_copy.wait()

    acc[...] = jnp.zeros_like(acc)
    tot[...] = jnp.zeros_like(tot)
    top[...] = jnp.full_like(top, LOW)
    scaling = q_ref.shape[2] ** -0.5

    def attend(g):
        begin = pl.multiple_of(g * span, span)
        at = pl.ds(begin, span)
        spot = half * ctx + begin + lax.broadcasted_iota(jnp.int32, (q_ref.shape[1], span), 1)
        for slot in range(SLOTS):
            own = slot // 2 == half
            asking = jnp.where(own, q_ref[slot % 2], q_peer[slot % 2])
            scores = (
                lax.dot_general(
                    asking,
                    mk_ref[slot, at, :],
                    (((1,), (1,)), ((), ())),
                    preferred_element_type=jnp.float32,
                )
                * scaling
            )
            usable = spot < table[SPAN + slot]
            before = top[slot][:, :1]
            highest = jnp.max(jnp.where(usable, scores, LOW), axis=1, keepdims=True)
            highest = jnp.maximum(highest, before)
            weights = jnp.where(usable, jnp.exp(scores - highest), 0.0)
            shrink = jnp.exp(before - highest)
            total = tot[slot][:, :1] * shrink + jnp.sum(weights, axis=1, keepdims=True)
            summed = jnp.dot(
                weights.astype(jnp.bfloat16),
                mv_ref[slot, at, :],
                preferred_element_type=jnp.float32,
            )
            acc[slot] = acc[slot] * shrink + summed
            top[slot] = jnp.broadcast_to(highest, top.shape[1:])
            tot[slot] = jnp.broadcast_to(total, tot.shape[1:])

    nearest = jnp.minimum(z, SIDE - 1 - z) * SKEW
    farthest = jnp.maximum(z, SIDE - 1 - z) * SKEW + cap - 1

    def on_group(t, late, act):
        g = (t - late) // cap

        @pl.when((t >= late) & ((t - late) % cap == 0) & (g < groups))
        def _():
            act(g)

    def x_arrive(g):
        for dx in range(1, SIDE):
            x_copy(g, dx).wait_recv()
            origin = (x + SIDE - dx) % SIDE
            for j in range(MOST):
                pool[g, origin * MOST + j] = x_in[g, dx - 1, j]

    def y_start(g):
        for dx in (1, 3, 2):
            to = (x + dx) % SIDE
            for j in range(MOST):
                y_out[g, dx - 1, j] = pool[g, table[OUT + to * MOST + j]]
            y_copy(g, dx).start()

    def settle(g):
        for dx in range(SIDE):
            origin = (x + SIDE - dx) % SIDE
            at = pl.ds(pl.multiple_of((g * SIDE + origin) * rows, rows), rows)
            if dx == 0:
                first = pool[g, table[OUT + x * MOST]]
                second = pool[g, table[OUT + x * MOST + 1]]
            else:
                y_copy(g, dx).wait_recv()
                first = y_in[g, dx - 1, 0]
                second = y_in[g, dx - 1, 1]
            for slot in range(SLOTS):
                sel = table[SEL + slot]
                for kv, (ref, out) in enumerate(((k_ref, mk_ref), (v_ref, mv_ref))):
                    piece = jnp.where(sel == 1, first[kv], ref[slot, at, :])
                    out[slot, at, :] = jnp.where(sel == 2, second[kv], piece)
        attend(g)

    def step(t, carry):
        on_group(t, nearest, x_arrive)
        k = t - z * SKEW

        @pl.when((k >= 0) & (k < units))
        def _():
            g, c = k // cap, k % cap

            @pl.when(z > 0)
            def _():
                up_copy(k).wait_recv()
                pool[g, ITEMS + c] = up_in[k]

            @pl.when(z < SIDE - 1)
            def _():
                up_out[k] = pool[g, table[UP + c]]
                up_copy(k).start()

        m = t - (SIDE - 1 - z) * SKEW

        @pl.when((m >= 0) & (m < units))
        def _():
            g, c = m // cap, m % cap

            @pl.when(z < SIDE - 1)
            def _():
                down_copy(m).wait_recv()
                pool[g, ITEMS + cap + c] = down_in[m]

            @pl.when(z > 0)
            def _():
                down_out[m] = pool[g, table[DOWN + c]]
                down_copy(m).start()

        on_group(t, farthest, y_start)
        on_group(t, farthest + LATER, settle)
        return carry

    lax.fori_loop(0, units + (SIDE - 1) * SKEW + LATER, step, 0)

    lane = lax.broadcasted_iota(jnp.int32, top.shape[1:], 1)
    for r in range(2):
        slot = (1 - half) * 2 + r
        p_out[r, 0] = acc[slot]
        p_out[r, 1] = jnp.where(lane < 64, top[slot], tot[slot])
    p_copy = pltpu.make_async_remote_copy(
        p_out, p_in, p_sem.at[0], p_sem.at[1], device_id=peer, device_id_type=MESH
    )
    p_copy.start()
    w_copy.wait()
    p_copy.wait_recv()
    news = fresh_ref.shape[1] // 2
    size = q_ref.shape[1] // news
    token = lax.broadcasted_iota(jnp.int32, (q_ref.shape[1], 1), 0) // size
    for r in range(2):
        slot = half * 2 + r
        top_a, tot_a = top[slot][:, :1], tot[slot][:, :1]
        top_b, tot_b = p_in[r, 1][:, :1], p_in[r, 1][:, 64:65]
        asking = q_ref[r].astype(jnp.float32)
        peak = jnp.maximum(top_a, top_b)
        fresh = []
        for m in range(news):
            score = jnp.sum(asking * fresh_ref[r, m : m + 1, :], axis=1, keepdims=True) * scaling
            score = jnp.where(token >= m, score, LOW)
            fresh.append(score)
            peak = jnp.maximum(peak, score)
        scale_a = jnp.exp(top_a - peak)
        scale_b = jnp.exp(top_b - peak)
        summed = acc[slot] * scale_a + p_in[r, 0] * scale_b
        total = tot_a * scale_a + tot_b * scale_b
        for m in range(news):
            weight = jnp.where(token >= m, jnp.exp(fresh[m] - peak), 0.0)
            total = total + weight
            summed = summed + weight * fresh_ref[r, news + m : news + m + 1, :]
        head[r] = summed / total
    for r in range(2):
        for a in range(size):
            for n in range(news):
                lhs[n * 2 + r : n * 2 + r + 1, a * 128 : (a + 1) * 128] = head[
                    r, n * size + a : n * size + a + 1, :
                ]
    left = lhs[...].astype(jnp.bfloat16)

    def s_copy(dt):
        return pltpu.make_async_remote_copy(
            s_out.at[dt],
            s_in.at[dt],
            s_send.at[dt],
            s_recv.at[dt],
            device_id=(inst, (tp + dt) % tps),
            device_id_type=MESH,
        )

    for dt in list(range(1, tps)) + [0]:
        to = (tp + dt) % tps
        part = jnp.dot(
            left,
            w_buf[:, pl.ds(pl.multiple_of(to * cols, cols), cols)],
            preferred_element_type=jnp.float32,
        )
        s_out[dt] = part
        if dt:
            s_copy(dt).start()
    mixed = s_out[0]
    for dt in range(1, tps):
        s_copy(dt).wait_recv()
        mixed = mixed + s_in[dt]
    mix_ref[...] = mixed.astype(jnp.bfloat16)

    q_done = [p_copy]
    for copy in q_done:
        copy.wait_send()
    for dt in range(1, tps):
        s_copy(dt).wait_send()

    def x_drain(g, carry):
        for dx in range(1, SIDE):
            x_copy(g, dx).wait_send()
            y_copy(g, dx).wait_send()
        return carry

    lax.fori_loop(0, groups, x_drain, 0)

    def z_drain(k, carry):
        @pl.when(z < SIDE - 1)
        def _():
            up_copy(k).wait_send()

        @pl.when(z > 0)
        def _():
            down_copy(k).wait_send()

        return carry

    lax.fori_loop(0, units, z_drain, 0)


def main_call(cap, collective_id, table, asking, fresh, keys, values, weight):
    slots, ctx, dim = keys.shape
    rows = ctx // (GROUPS * SIDE)
    tps = lax.axis_size("tp")
    cols = weight.shape[1] // tps
    queries = asking.shape[1]
    unit = (2, rows, dim)
    units = GROUPS * cap
    bf16, f32 = jnp.bfloat16, jnp.float32
    vmem = pl.BlockSpec(memory_space=pltpu.VMEM)
    spread = pltpu.VMEM((GROUPS, SIDE - 1, MOST) + unit, bf16)
    line = pltpu.VMEM((units,) + unit, bf16)
    dma = pltpu.SemaphoreType.DMA
    return pl.pallas_call(
        functools.partial(main_kernel, cap),
        out_shape=(
            jax.ShapeDtypeStruct(keys.shape, bf16),
            jax.ShapeDtypeStruct(values.shape, bf16),
            jax.ShapeDtypeStruct((asking.shape[0] * fresh.shape[1] // 2, cols), bf16),
        ),
        in_specs=[
            pl.BlockSpec(memory_space=pltpu.SMEM),
            vmem,
            vmem,
            vmem,
            vmem,
            pl.BlockSpec(memory_space=pl.ANY),
        ],
        out_specs=(vmem, vmem, vmem),
        scratch_shapes=[
            pltpu.VMEM(weight.shape, bf16),
            pltpu.VMEM(asking.shape, bf16),
            spread,
            spread,
            pltpu.VMEM((GROUPS, ITEMS + 2 * cap) + unit, bf16),
            line,
            line,
            line,
            line,
            spread,
            spread,
            pltpu.VMEM((slots, queries, dim), f32),
            pltpu.VMEM((slots, queries, dim), f32),
            pltpu.VMEM((slots, queries, dim), f32),
            pltpu.VMEM((2, 2, queries, dim), f32),
            pltpu.VMEM((2, 2, queries, dim), f32),
            pltpu.VMEM((2, queries, dim), f32),
            pltpu.VMEM((8, weight.shape[0]), f32),
            pltpu.VMEM((tps, 8, cols), f32),
            pltpu.VMEM((tps, 8, cols), f32),
            dma,
            dma((2,)),
            dma((GROUPS, SIDE - 1)),
            dma((GROUPS, SIDE - 1)),
            dma((units,)),
            dma((units,)),
            dma((units,)),
            dma((units,)),
            dma((GROUPS, SIDE - 1)),
            dma((GROUPS, SIDE - 1)),
            dma((2,)),
            dma((tps,)),
            dma((tps,)),
        ],
        compiler_params=pltpu.CompilerParams(
            collective_id=collective_id, has_side_effects=True, vmem_limit_bytes=56 << 20
        ),
        name=f"move_attend_{cap}",
    )(table, asking, fresh, keys, values, weight)


def on_device(
    keys_cache,
    values_cache,
    queries,
    fresh_keys,
    fresh_values,
    out_weight,
    partner,
    chosen,
    lengths,
    dest_slot,
):
    _, slots, ctx, _, dim = keys_cache.shape
    news, own = queries.shape[:2]
    size = queries.shape[2] // dim
    smem = pl.BlockSpec(memory_space=pltpu.SMEM)
    table = pl.pallas_call(
        plan_kernel,
        out_shape=jax.ShapeDtypeStruct((TABLE,), jnp.int32),
        in_specs=[smem] * 4,
        out_specs=smem,
        scratch_shapes=[pltpu.SMEM((16,), jnp.int32), pltpu.SMEM((16,), jnp.int32)],
        name="plan",
    )(partner, chosen.T, lengths.T, dest_slot.T)
    asking = queries.reshape(news, own, size, dim).transpose(1, 0, 2, 3)
    asking = asking.reshape(own, news * size, dim)
    fresh = jnp.concatenate([fresh_keys, fresh_values], axis=0).transpose(1, 0, 2)
    fresh = fresh.astype(jnp.float32)
    keys = keys_cache.reshape(slots, ctx, dim)
    values = values_cache.reshape(slots, ctx, dim)
    args = (table, asking, fresh, keys, values, out_weight)
    if len(CAPS) == 1:
        moved_keys, moved_values, mixed = main_call(CAPS[0], 0, *args)
    else:
        moved_keys, moved_values, mixed = lax.switch(
            table[WHICH],
            [functools.partial(main_call, cap, i) for i, cap in enumerate(CAPS)],
            *args,
        )
    return (
        moved_keys.reshape(keys_cache.shape),
        moved_values.reshape(values_cache.shape),
        mixed.reshape(news, own, mixed.shape[1]),
    )


def solution(mesh):
    in_specs = (
        P("inst", None, None, "tp", None),
        P("inst", None, None, "tp", None),
        P(None, "inst", "tp"),
        P(None, "inst", "tp"),
        P(None, "inst", "tp"),
        P("tp", None),
        P(),
        P(),
        P(),
        P(),
    )
    out_specs = (
        P("inst", None, None, "tp", None),
        P("inst", None, None, "tp", None),
        P(None, "inst", "tp"),
    )
    return jax.shard_map(
        on_device, mesh=mesh, in_specs=in_specs, out_specs=out_specs, check_vma=False
    )
```

```python
import functools

import jax
import jax.numpy as jnp
from jax import lax
from jax.experimental import pallas as pl
from jax.experimental.pallas import tpu as pltpu
from jax.sharding import PartitionSpec as P

MESH = pl.DeviceIdType.MESH
LOW = -1e30
SLOTS = 4
MOST = 2
SIDE = 4
ITEMS = SIDE * MOST
WIDEST = ITEMS * 2
CAPS = (5, 6, 7, 8, 10, 16)
GROUPS = 4
SKEW = 4
LATER = 4
UP, DOWN, OUT, SEL, SPAN, PICK, NONE, WHICH, TABLE = 0, 16, 32, 40, 44, 48, 50, 51, 64


def where_am_i():
    inst = lax.axis_index("inst")
    chip = inst // 2
    return inst % 2, chip, chip // SIDE, chip % SIDE


def plan_kernel(partner, chosen, lengths, dest, table, count, start):
    _, me, _, z = where_am_i()
    sent = []
    for i in range(16):
        count[i] = 0
    for s in range(16):
        sent.append(sum(chosen[r, s] for r in range(SLOTS)))
        cls = (s % SIDE) * SIDE + partner[s] % SIDE
        count[cls] = count[cls] + sent[s]
    n = [[count[a * SIDE + b] for b in range(SIDE)] for a in range(SIDE)]

    def flip(a, b, down):
        return n[3 - a][3 - b] if down else n[a][b]

    need = 0
    for down in (False, True):
        f = functools.partial(flip, down=down)
        need = functools.reduce(
            jnp.maximum,
            (
                need,
                f(0, 1) + f(0, 2) + f(0, 3),
                f(0, 2) + f(0, 3) + f(1, 2) + f(1, 3),
                f(0, 3) + f(1, 3) + f(2, 3),
            ),
        )
    which, cap = 0, CAPS[0]
    for i in range(1, len(CAPS)):
        which = jnp.where(need > CAPS[i - 1], i, which)
        cap = jnp.where(need > CAPS[i - 1], CAPS[i], cap)
    for down in (False, True):
        f = functools.partial(flip, down=down)
        places = {
            (0, 3): 0,
            (1, 3): f(0, 3),
            (1, 2): f(0, 3) + f(1, 3),
            (0, 2): cap - f(0, 2),
            (0, 1): f(0, 3),
            (2, 3): f(0, 3) + f(1, 3),
        }
        for (a, b), place in places.items():
            start[(3 - a) * SIDE + 3 - b if down else a * SIDE + b] = place
    for a in range(SIDE):
        start[a * SIDE + a] = 0
    for c in range(WIDEST):
        table[UP + c] = jnp.where(z == 0, 0, ITEMS + c)
        table[DOWN + c] = jnp.where(z == SIDE - 1, 0, ITEMS + cap + c)
    for i in range(OUT, TABLE):
        table[i] = 0
    source = 0
    for s in range(16):
        d = partner[s]
        source = jnp.where(d == me, s, source)
        zs, xs = s % SIDE, s // SIDE
        zd, xd = d % SIDE, d // SIDE
        base = start[zs * SIDE + zd]
        start[zs * SIDE + zd] = base + sent[s]
        for j in range(MOST):
            valid = j < sent[s]
            leaves = valid & (zs == z) & (zd != zs)
            place = jnp.where(zd > zs, UP, DOWN) + base + j
            table[jnp.where(leaves, place, NONE)] = xs * MOST + j
            lands = valid & (zd == z)
            kept = jnp.where(zs < z, ITEMS + base + j, ITEMS + cap + base + j)
            kept = jnp.where(zs == z, xs * MOST + j, kept)
            table[jnp.where(lands, OUT + xd * MOST + j, NONE)] = kept
    mine, theirs = 0, 0
    for r in range(SLOTS):
        table[SPAN + r] = lengths[r, me]
    for r in range(SLOTS):
        go = chosen[r, me] == 1
        table[jnp.where(go, PICK + mine, NONE)] = r
        mine = mine + jnp.where(go, 1, 0)
        come = chosen[r, source] == 1
        slot = dest[r, source]
        theirs = theirs + jnp.where(come, 1, 0)
        table[jnp.where(come, SEL + slot, NONE)] = theirs
        table[jnp.where(come, SPAN + slot, NONE)] = lengths[r, source]
    table[WHICH] = which


def main_kernel(
    cap,
    table,
    q_ref,
    fresh_ref,
    k_ref,
    v_ref,
    w_hbm,
    mk_ref,
    mv_ref,
    mix_ref,
    w_buf,
    q_peer,
    x_out,
    x_in,
    pool,
    up_out,
    up_in,
    down_out,
    down_in,
    y_out,
    y_in,
    acc,
    top,
    tot,
    p_out,
    p_in,
    head,
    lhs,
    s_out,
    s_in,
    w_sem,
    q_sem,
    x_send,
    x_recv,
    up_send,
    up_recv,
    down_send,
    down_recv,
    y_send,
    y_recv,
    p_sem,
    s_send,
    s_recv,
):
    groups = x_out.shape[0]
    rows = x_out.shape[4]
    ctx = k_ref.shape[1]
    span = ctx // groups
    tps = s_out.shape[0]
    cols = s_out.shape[2]
    units = groups * cap
    half, chip, x, z = where_am_i()
    inst = lax.axis_index("inst")
    tp = lax.axis_index("tp")
    peer = (inst + 1 - 2 * half, tp)

    def along_x(dx):
        return (((x + dx) % SIDE * SIDE + z) * 2 + half, tp)

    above = (inst + 2, tp)
    below = (inst - 2, tp)

    barrier = pltpu.get_barrier_semaphore()

    def greet(device):
        pl.semaphore_signal(barrier, inc=1, device_id=device, device_id_type=MESH)

    greet(peer)
    for dx in range(1, SIDE):
        greet(along_x(dx))
    for dt in range(1, tps):
        greet((inst, (tp + dt) % tps))

    @pl.when(z < SIDE - 1)
    def _():
        greet(above)

    @pl.when(z > 0)
    def _():
        greet(below)

    w_copy = pltpu.make_async_copy(w_hbm, w_buf, w_sem)
    w_copy.start()

    def stage(g, carry):
        for dx in range(SIDE):
            to = (x + dx) % SIDE
            at = pl.ds(pl.multiple_of((g * SIDE + to) * rows, rows), rows)
            for j in range(MOST):
                slot = table[PICK + j]
                for kv, ref in enumerate((k_ref, v_ref)):
                    piece = ref[slot, at, :]
                    if dx == 0:
                        pool[g, x * MOST + j, kv] = piece
                    else:
                        x_out[g, dx - 1, j, kv] = piece
        return carry

    lax.fori_loop(0, groups, stage, 0)
    peers = 1 + (SIDE - 1) + (tps - 1)
    pl.semaphore_wait(
        barrier, peers + jnp.where(z > 0, 1, 0) + jnp.where(z < SIDE - 1, 1, 0)
    )

    q_copy = pltpu.make_async_remote_copy(
        q_ref, q_peer, q_sem.at[0], q_sem.at[1], device_id=peer, device_id_type=MESH
    )
    q_copy.start()

    def x_copy(g, dx):
        return pltpu.make_async_remote_copy(
            x_out.at[g, dx - 1],
            x_in.at[g, dx - 1],
            x_send.at[g, dx - 1],
            x_recv.at[g, dx - 1],
            device_id=along_x(dx),
            device_id_type=MESH,
        )

    def y_copy(g, dx):
        return pltpu.make_async_remote_copy(
            y_out.at[g, dx - 1],
            y_in.at[g, dx - 1],
            y_send.at[g, dx - 1],
            y_recv.at[g, dx - 1],
            device_id=along_x(dx),
            device_id_type=MESH,
        )

    def up_copy(k):
        return pltpu.make_async_remote_copy(
            up_out.at[k],
            up_in.at[k],
            up_send.at[k],
            up_recv.at[k],
            device_id=above,
            device_id_type=MESH,
        )

    def down_copy(k):
        return pltpu.make_async_remote_copy(
            down_out.at[k],
            down_in.at[k],
            down_send.at[k],
            down_recv.at[k],
            device_id=below,
            device_id_type=MESH,
        )

    def x_start(g, carry):
        for dx in (1, 3, 2):
            x_copy(g, dx).start()
        return carry

    lax.fori_loop(0, groups, x_start, 0)
    q_copy.wait()

    acc[...] = jnp.zeros_like(acc)
    tot[...] = jnp.zeros_like(tot)
    top[...] = jnp.full_like(top, LOW)
    scaling = q_ref.shape[2] ** -0.5

    def attend(g):
        begin = pl.multiple_of(g * span, span)
        at = pl.ds(begin, span)
        spot = half * ctx + begin + lax.broadcasted_iota(jnp.int32, (q_ref.shape[1], span), 1)
        for slot in range(SLOTS):
            own = slot // 2 == half
            asking = jnp.where(own, q_ref[slot % 2], q_peer[slot % 2])
            scores = (
                lax.dot_general(
                    asking,
                    mk_ref[slot, at, :],
                    (((1,), (1,)), ((), ())),
                    preferred_element_type=jnp.float32,
                )
                * scaling
            )
            usable = spot < table[SPAN + slot]
            before = top[slot][:, :1]
            highest = jnp.max(jnp.where(usable, scores, LOW), axis=1, keepdims=True)
            highest = jnp.maximum(highest, before)
            weights = jnp.where(usable, jnp.exp(scores - highest), 0.0)
            shrink = jnp.exp(before - highest)
            total = tot[slot][:, :1] * shrink + jnp.sum(weights, axis=1, keepdims=True)
            summed = jnp.dot(
                weights.astype(jnp.bfloat16),
                mv_ref[slot, at, :],
                preferred_element_type=jnp.float32,
            )
            acc[slot] = acc[slot] * shrink + summed
            top[slot] = jnp.broadcast_to(highest, top.shape[1:])
            tot[slot] = jnp.broadcast_to(total, tot.shape[1:])

    nearest = jnp.minimum(z, SIDE - 1 - z) * SKEW
    farthest = jnp.maximum(z, SIDE - 1 - z) * SKEW + cap - 1

    def on_group(t, late, act):
        g = (t - late) // cap

        @pl.when((t >= late) & ((t - late) % cap == 0) & (g < groups))
        def _():
            act(g)

    def x_arrive(g):
        for dx in range(1, SIDE):
            x_copy(g, dx).wait_recv()
            origin = (x + SIDE - dx) % SIDE
            for j in range(MOST):
                pool[g, origin * MOST + j] = x_in[g, dx - 1, j]

    def y_start(g):
        for dx in (1, 3, 2):
            to = (x + dx) % SIDE
            for j in range(MOST):
                y_out[g, dx - 1, j] = pool[g, table[OUT + to * MOST + j]]
            y_copy(g, dx).start()

    def settle(g):
        for dx in range(SIDE):
            origin = (x + SIDE - dx) % SIDE
            at = pl.ds(pl.multiple_of((g * SIDE + origin) * rows, rows), rows)
            if dx == 0:
                first = pool[g, table[OUT + x * MOST]]
                second = pool[g, table[OUT + x * MOST + 1]]
            else:
                y_copy(g, dx).wait_recv()
                first = y_in[g, dx - 1, 0]
                second = y_in[g, dx - 1, 1]
            for slot in range(SLOTS):
                sel = table[SEL + slot]
                for kv, (ref, out) in enumerate(((k_ref, mk_ref), (v_ref, mv_ref))):
                    piece = jnp.where(sel == 1, first[kv], ref[slot, at, :])
                    out[slot, at, :] = jnp.where(sel == 2, second[kv], piece)
        attend(g)

    def step(t, carry):
        on_group(t, nearest, x_arrive)
        k = t - z * SKEW

        @pl.when((k >= 0) & (k < units))
        def _():
            g, c = k // cap, k % cap

            @pl.when(z > 0)
            def _():
                up_copy(k).wait_recv()
                pool[g, ITEMS + c] = up_in[k]

            @pl.when(z < SIDE - 1)
            def _():
                up_out[k] = pool[g, table[UP + c]]
                up_copy(k).start()

        m = t - (SIDE - 1 - z) * SKEW

        @pl.when((m >= 0) & (m < units))
        def _():
            g, c = m // cap, m % cap

            @pl.when(z < SIDE - 1)
            def _():
                down_copy(m).wait_recv()
                pool[g, ITEMS + cap + c] = down_in[m]

            @pl.when(z > 0)
            def _():
                down_out[m] = pool[g, table[DOWN + c]]
                down_copy(m).start()

        on_group(t, farthest, y_start)
        on_group(t, farthest + LATER, settle)
        return carry

    lax.fori_loop(0, units + (SIDE - 1) * SKEW + LATER, step, 0)

    lane = lax.broadcasted_iota(jnp.int32, top.shape[1:], 1)
    for r in range(2):
        slot = (1 - half) * 2 + r
        p_out[r, 0] = acc[slot]
        p_out[r, 1] = jnp.where(lane < 64, top[slot], tot[slot])
    p_copy = pltpu.make_async_remote_copy(
        p_out, p_in, p_sem.at[0], p_sem.at[1], device_id=peer, device_id_type=MESH
    )
    p_copy.start()
    w_copy.wait()
    p_copy.wait_recv()
    news = fresh_ref.shape[1] // 2
    size = q_ref.shape[1] // news
    token = lax.broadcasted_iota(jnp.int32, (q_ref.shape[1], 1), 0) // size
    for r in range(2):
        slot = half * 2 + r
        top_a, tot_a = top[slot][:, :1], tot[slot][:, :1]
        top_b, tot_b = p_in[r, 1][:, :1], p_in[r, 1][:, 64:65]
        asking = q_ref[r].astype(jnp.float32)
        peak = jnp.maximum(top_a, top_b)
        fresh = []
        for m in range(news):
            score = jnp.sum(asking * fresh_ref[r, m : m + 1, :], axis=1, keepdims=True) * scaling
            score = jnp.where(token >= m, score, LOW)
            fresh.append(score)
            peak = jnp.maximum(peak, score)
        scale_a = jnp.exp(top_a - peak)
        scale_b = jnp.exp(top_b - peak)
        summed = acc[slot] * scale_a + p_in[r, 0] * scale_b
        total = tot_a * scale_a + tot_b * scale_b
        for m in range(news):
            weight = jnp.where(token >= m, jnp.exp(fresh[m] - peak), 0.0)
            total = total + weight
            summed = summed + weight * fresh_ref[r, news + m : news + m + 1, :]
        head[r] = summed / total
    for r in range(2):
        for a in range(size):
            for n in range(news):
                lhs[n * 2 + r : n * 2 + r + 1, a * 128 : (a + 1) * 128] = head[
                    r, n * size + a : n * size + a + 1, :
                ]
    left = lhs[...].astype(jnp.bfloat16)

    def s_copy(dt):
        return pltpu.make_async_remote_copy(
            s_out.at[dt],
            s_in.at[dt],
            s_send.at[dt],
            s_recv.at[dt],
            device_id=(inst, (tp + dt) % tps),
            device_id_type=MESH,
        )

    for dt in list(range(1, tps)) + [0]:
        to = (tp + dt) % tps
        part = jnp.dot(
            left,
            w_buf[:, pl.ds(pl.multiple_of(to * cols, cols), cols)],
            preferred_element_type=jnp.float32,
        )
        s_out[dt] = part
        if dt:
            s_copy(dt).start()
    mixed = s_out[0]
    for dt in range(1, tps):
        s_copy(dt).wait_recv()
        mixed = mixed + s_in[dt]
    mix_ref[...] = mixed.astype(jnp.bfloat16)

    q_done = [p_copy]
    for copy in q_done:
        copy.wait_send()
    for dt in range(1, tps):
        s_copy(dt).wait_send()

    def x_drain(g, carry):
        for dx in range(1, SIDE):
            x_copy(g, dx).wait_send()
            y_copy(g, dx).wait_send()
        return carry

    lax.fori_loop(0, groups, x_drain, 0)

    def z_drain(k, carry):
        @pl.when(z < SIDE - 1)
        def _():
            up_copy(k).wait_send()

        @pl.when(z > 0)
        def _():
            down_copy(k).wait_send()

        return carry

    lax.fori_loop(0, units, z_drain, 0)


def main_call(cap, collective_id, table, asking, fresh, keys, values, weight):
    slots, ctx, dim = keys.shape
    rows = ctx // (GROUPS * SIDE)
    tps = lax.axis_size("tp")
    cols = weight.shape[1] // tps
    queries = asking.shape[1]
    unit = (2, rows, dim)
    units = GROUPS * cap
    bf16, f32 = jnp.bfloat16, jnp.float32
    vmem = pl.BlockSpec(memory_space=pltpu.VMEM)
    spread = pltpu.VMEM((GROUPS, SIDE - 1, MOST) + unit, bf16)
    line = pltpu.VMEM((units,) + unit, bf16)
    dma = pltpu.SemaphoreType.DMA
    return pl.pallas_call(
        functools.partial(main_kernel, cap),
        out_shape=(
            jax.ShapeDtypeStruct(keys.shape, bf16),
            jax.ShapeDtypeStruct(values.shape, bf16),
            jax.ShapeDtypeStruct((asking.shape[0] * fresh.shape[1] // 2, cols), bf16),
        ),
        in_specs=[
            pl.BlockSpec(memory_space=pltpu.SMEM),
            vmem,
            vmem,
            vmem,
            vmem,
            pl.BlockSpec(memory_space=pl.ANY),
        ],
        out_specs=(vmem, vmem, vmem),
        scratch_shapes=[
            pltpu.VMEM(weight.shape, bf16),
            pltpu.VMEM(asking.shape, bf16),
            spread,
            spread,
            pltpu.VMEM((GROUPS, ITEMS + 2 * cap) + unit, bf16),
            line,
            line,
            line,
            line,
            spread,
            spread,
            pltpu.VMEM((slots, queries, dim), f32),
            pltpu.VMEM((slots, queries, dim), f32),
            pltpu.VMEM((slots, queries, dim), f32),
            pltpu.VMEM((2, 2, queries, dim), f32),
            pltpu.VMEM((2, 2, queries, dim), f32),
            pltpu.VMEM((2, queries, dim), f32),
            pltpu.VMEM((8, weight.shape[0]), f32),
            pltpu.VMEM((tps, 8, cols), f32),
            pltpu.VMEM((tps, 8, cols), f32),
            dma,
            dma((2,)),
            dma((GROUPS, SIDE - 1)),
            dma((GROUPS, SIDE - 1)),
            dma((units,)),
            dma((units,)),
            dma((units,)),
            dma((units,)),
            dma((GROUPS, SIDE - 1)),
            dma((GROUPS, SIDE - 1)),
            dma((2,)),
            dma((tps,)),
            dma((tps,)),
        ],
        compiler_params=pltpu.CompilerParams(
            collective_id=collective_id, has_side_effects=True, vmem_limit_bytes=56 << 20
        ),
        name=f"move_attend_{cap}",
    )(table, asking, fresh, keys, values, weight)


def on_device(
    keys_cache,
    values_cache,
    queries,
    fresh_keys,
    fresh_values,
    out_weight,
    partner,
    chosen,
    lengths,
    dest_slot,
):
    _, slots, ctx, _, dim = keys_cache.shape
    news, own = queries.shape[:2]
    size = queries.shape[2] // dim
    smem = pl.BlockSpec(memory_space=pltpu.SMEM)
    table = pl.pallas_call(
        plan_kernel,
        out_shape=jax.ShapeDtypeStruct((TABLE,), jnp.int32),
        in_specs=[smem] * 4,
        out_specs=smem,
        scratch_shapes=[pltpu.SMEM((16,), jnp.int32), pltpu.SMEM((16,), jnp.int32)],
        name="plan",
    )(partner, chosen.T, lengths.T, dest_slot.T)
    asking = queries.reshape(news, own, size, dim).transpose(1, 0, 2, 3)
    asking = asking.reshape(own, news * size, dim)
    fresh = jnp.concatenate([fresh_keys, fresh_values], axis=0).transpose(1, 0, 2)
    fresh = fresh.astype(jnp.float32)
    keys = keys_cache.reshape(slots, ctx, dim)
    values = values_cache.reshape(slots, ctx, dim)
    args = (table, asking, fresh, keys, values, out_weight)
    if len(CAPS) == 1:
        moved_keys, moved_values, mixed = main_call(CAPS[0], 0, *args)
    else:
        moved_keys, moved_values, mixed = lax.switch(
            table[WHICH],
            [functools.partial(main_call, cap, i) for i, cap in enumerate(CAPS)],
            *args,
        )
    return (
        moved_keys.reshape(keys_cache.shape),
        moved_values.reshape(values_cache.shape),
        mixed.reshape(news, own, mixed.shape[1]),
    )


def solution(mesh):
    in_specs = (
        P("inst", None, None, "tp", None),
        P("inst", None, None, "tp", None),
        P(None, "inst", "tp"),
        P(None, "inst", "tp"),
        P(None, "inst", "tp"),
        P("tp", None),
        P(),
        P(),
        P(),
        P(),
    )
    out_specs = (
        P("inst", None, None, "tp", None),
        P("inst", None, None, "tp", None),
        P(None, "inst", "tp"),
    )
    return jax.shard_map(
        on_device, mesh=mesh, in_specs=in_specs, out_specs=out_specs, check_vma=False
    )
```

```python
import functools

import jax
import jax.numpy as jnp
from jax import lax
from jax.experimental import pallas as pl
from jax.experimental.pallas import tpu as pltpu
from jax.sharding import PartitionSpec as P

MESH = pl.DeviceIdType.MESH
LOW = -1e30
SLOTS = 4
MOST = 2
SIDE = 4
ITEMS = SIDE * MOST
WIDEST = ITEMS * 2
CAPS = (5, 6, 7, 8, 10, 16)
GROUPS = 4
SKEW = 6
UP, DOWN, OUT, SEL, SPAN, PICK, NONE, WHICH, TABLE = 0, 16, 32, 40, 44, 48, 50, 51, 64


def where_am_i():
    inst = lax.axis_index("inst")
    chip = inst // 2
    return inst % 2, chip, chip // SIDE, chip % SIDE


def plan_kernel(partner, chosen, lengths, dest, table, count, start):
    _, me, _, z = where_am_i()
    sent = []
    for i in range(16):
        count[i] = 0
    for s in range(16):
        sent.append(sum(chosen[r, s] for r in range(SLOTS)))
        cls = (s % SIDE) * SIDE + partner[s] % SIDE
        count[cls] = count[cls] + sent[s]
    n = [[count[a * SIDE + b] for b in range(SIDE)] for a in range(SIDE)]

    def flip(a, b, down):
        return n[3 - a][3 - b] if down else n[a][b]

    need = 0
    for down in (False, True):
        f = functools.partial(flip, down=down)
        need = functools.reduce(
            jnp.maximum,
            (
                need,
                f(0, 1) + f(0, 2) + f(0, 3),
                f(0, 2) + f(0, 3) + f(1, 2) + f(1, 3),
                f(0, 3) + f(1, 3) + f(2, 3),
            ),
        )
    which, cap = 0, CAPS[0]
    for i in range(1, len(CAPS)):
        which = jnp.where(need > CAPS[i - 1], i, which)
        cap = jnp.where(need > CAPS[i - 1], CAPS[i], cap)
    for down in (False, True):
        f = functools.partial(flip, down=down)
        places = {
            (0, 3): 0,
            (1, 3): f(0, 3),
            (1, 2): f(0, 3) + f(1, 3),
            (0, 2): cap - f(0, 2),
            (0, 1): f(0, 3),
            (2, 3): f(0, 3) + f(1, 3),
        }
        for (a, b), place in places.items():
            start[(3 - a) * SIDE + 3 - b if down else a * SIDE + b] = place
    for a in range(SIDE):
        start[a * SIDE + a] = 0
    for c in range(WIDEST):
        table[UP + c] = jnp.where(z == 0, 0, ITEMS + c)
        table[DOWN + c] = jnp.where(z == SIDE - 1, 0, ITEMS + cap + c)
    for i in range(OUT, TABLE):
        table[i] = 0
    source = 0
    for s in range(16):
        d = partner[s]
        source = jnp.where(d == me, s, source)
        zs, xs = s % SIDE, s // SIDE
        zd, xd = d % SIDE, d // SIDE
        base = start[zs * SIDE + zd]
        start[zs * SIDE + zd] = base + sent[s]
        for j in range(MOST):
            valid = j < sent[s]
            leaves = valid & (zs == z) & (zd != zs)
            place = jnp.where(zd > zs, UP, DOWN) + base + j
            table[jnp.where(leaves, place, NONE)] = xs * MOST + j
            lands = valid & (zd == z)
            kept = jnp.where(zs < z, ITEMS + base + j, ITEMS + cap + base + j)
            kept = jnp.where(zs == z, xs * MOST + j, kept)
            table[jnp.where(lands, OUT + xd * MOST + j, NONE)] = kept
    mine, theirs = 0, 0
    for r in range(SLOTS):
        table[SEL + r] = r
        table[SPAN + r] = lengths[r, me]
    for r in range(SLOTS):
        go = chosen[r, me] == 1
        table[jnp.where(go, PICK + mine, NONE)] = r
        mine = mine + jnp.where(go, 1, 0)
        come = chosen[r, source] == 1
        slot = dest[r, source]
        theirs = theirs + jnp.where(come, 1, 0)
        table[jnp.where(come, SEL + slot, NONE)] = SLOTS - 1 + theirs
        table[jnp.where(come, SPAN + slot, NONE)] = lengths[r, source]
    table[WHICH] = which


def main_kernel(
    cap,
    table,
    raw_ref,
    fk_ref,
    fv_ref,
    k_hbm,
    v_hbm,
    w_hbm,
    mk_ref,
    mv_ref,
    mix_ref,
    w_buf,
    k_ref,
    v_ref,
    q_rows,
    q_ref,
    q_peer,
    x_out,
    x_in,
    pool,
    up_out,
    up_in,
    down_out,
    down_in,
    y_out,
    y_in,
    acc,
    top,
    tot,
    p_out,
    p_in,
    head,
    lhs,
    s_out,
    s_in,
    w_sem,
    kv_sem,
    q_sem,
    x_send,
    x_recv,
    up_send,
    up_recv,
    down_send,
    down_recv,
    y_send,
    y_recv,
    p_sem,
    s_send,
    s_recv,
):
    groups = x_out.shape[0]
    rows = x_out.shape[4]
    ctx = k_ref.shape[1]
    span = ctx // groups
    tps = s_out.shape[0]
    cols = mix_ref.shape[1]
    wide = cols // 2
    units = groups * cap
    news, _, width = raw_ref.shape
    dim = k_ref.shape[2]
    size = width // dim
    half, chip, x, z = where_am_i()
    inst = lax.axis_index("inst")
    tp = lax.axis_index("tp")
    peer = (inst + 1 - 2 * half, tp)

    def along_x(dx):
        return (((x + dx) % SIDE * SIDE + z) * 2 + half, tp)

    above = (inst + 2, tp)
    below = (inst - 2, tp)

    k_copy = pltpu.make_async_copy(k_hbm, k_ref.at[:SLOTS], kv_sem.at[0])
    v_copy = pltpu.make_async_copy(v_hbm, v_ref.at[:SLOTS], kv_sem.at[1])
    k_copy.start()
    v_copy.start()
    barrier = pltpu.get_barrier_semaphore()

    def greet(device):
        pl.semaphore_signal(barrier, inc=1, device_id=device, device_id_type=MESH)

    greet(peer)
    for dx in range(1, SIDE):
        greet(along_x(dx))
    for dt in range(1, tps):
        greet((inst, (tp + dt) % tps))

    @pl.when(z < SIDE - 1)
    def _():
        greet(above)

    @pl.when(z > 0)
    def _():
        greet(below)

    w_copy = pltpu.make_async_copy(w_hbm, w_buf, w_sem)
    k_copy.wait()
    v_copy.wait()

    def stage(g, carry):
        for dx in range(SIDE):
            to = (x + dx) % SIDE
            at = pl.ds(pl.multiple_of((g * SIDE + to) * rows, rows), rows)
            for j in range(MOST):
                slot = table[PICK + j]
                for kv, ref in enumerate((k_ref, v_ref)):
                    piece = ref[slot, at, :]
                    if dx == 0:
                        pool[g, x * MOST + j, kv] = piece
                    else:
                        x_out[g, dx - 1, j, kv] = piece
        return carry

    stage(0, 0)
    peers = 1 + (SIDE - 1) + (tps - 1)
    pl.semaphore_wait(
        barrier, peers + jnp.where(z > 0, 1, 0) + jnp.where(z < SIDE - 1, 1, 0)
    )

    def x_copy(g, dx):
        return pltpu.make_async_remote_copy(
            x_out.at[g, dx - 1],
            x_in.at[g, dx - 1],
            x_send.at[g, dx - 1],
            x_recv.at[g, dx - 1],
            device_id=along_x(dx),
            device_id_type=MESH,
        )

    def y_copy(g, dx):
        return pltpu.make_async_remote_copy(
            y_out.at[g, dx - 1],
            y_in.at[g, dx - 1],
            y_send.at[g, dx - 1],
            y_recv.at[g, dx - 1],
            device_id=along_x(dx),
            device_id_type=MESH,
        )

    def up_copy(k):
        return pltpu.make_async_remote_copy(
            up_out.at[k],
            up_in.at[k],
            up_send.at[k],
            up_recv.at[k],
            device_id=above,
            device_id_type=MESH,
        )

    def down_copy(k):
        return pltpu.make_async_remote_copy(
            down_out.at[k],
            down_in.at[k],
            down_send.at[k],
            down_recv.at[k],
            device_id=below,
            device_id_type=MESH,
        )

    def x_start(g):
        for dx in (1, 3, 2):
            x_copy(g, dx).start()

    x_start(0)

    def x_rest(g, carry):
        stage(g, carry)
        x_start(g)
        return carry

    lax.fori_loop(1, groups, x_rest, 0)
    w_copy.start()
    for n in range(news):
        raw = raw_ref[n].astype(jnp.float32)
        for r in range(2):
            for a in range(size):
                q_rows[r, n * size + a : n * size + a + 1, :] = raw[
                    r : r + 1, a * dim : (a + 1) * dim
                ]
    for r in range(2):
        q_ref[r] = q_rows[r].astype(jnp.bfloat16)
    q_copy = pltpu.make_async_remote_copy(
        q_ref, q_peer, q_sem.at[0], q_sem.at[1], device_id=peer, device_id_type=MESH
    )
    q_copy.start()
    acc[...] = jnp.zeros_like(acc)
    tot[...] = jnp.zeros_like(tot)
    top[...] = jnp.full_like(top, LOW)
    scaling = dim**-0.5
    q_copy.wait()

    def attend(g, slot):
        begin = pl.multiple_of(g * span, span)
        at = pl.ds(begin, span)
        spot = half * ctx + begin + lax.broadcasted_iota(jnp.int32, (q_ref.shape[1], span), 1)
        own = slot // 2 == half
        source = table[SEL + slot]
        keys, values = k_ref[source, at, :], v_ref[source, at, :]
        mk_ref[slot, at, :] = keys
        mv_ref[slot, at, :] = values
        asking = jnp.where(own, q_ref[slot % 2], q_peer[slot % 2])
        scores = (
            lax.dot_general(
                asking,
                keys,
                (((1,), (1,)), ((), ())),
                preferred_element_type=jnp.float32,
            )
            * scaling
        )
        usable = spot < table[SPAN + slot]
        before = top[slot][:, :1]
        highest = jnp.max(jnp.where(usable, scores, LOW), axis=1, keepdims=True)
        highest = jnp.maximum(highest, before)
        weights = jnp.where(usable, jnp.exp(scores - highest), 0.0)
        shrink = jnp.exp(before - highest)
        total = tot[slot][:, :1] * shrink + jnp.sum(weights, axis=1, keepdims=True)
        summed = jnp.dot(
            weights.astype(jnp.bfloat16),
            values,
            preferred_element_type=jnp.float32,
        )
        acc[slot] = acc[slot] * shrink + summed
        top[slot] = jnp.broadcast_to(highest, top.shape[1:])
        tot[slot] = jnp.broadcast_to(total, tot.shape[1:])

    nearest = jnp.minimum(z, SIDE - 1 - z) * SKEW
    farthest = jnp.maximum(z, SIDE - 1 - z) * SKEW + cap - 1

    factor = -(-(1 << 16) // cap)

    def split(k):
        g = lax.shift_right_arithmetic(k * factor, 16)
        return g, k - g * cap

    def x_arrive(g):
        for dx in range(1, SIDE):
            x_copy(g, dx).wait_recv()
            origin = (x + SIDE - dx) % SIDE
            for j in range(MOST):
                pool[g, origin * MOST + j] = x_in[g, dx - 1, j]

    def y_start(g):
        for dx in (1, 3, 2):
            to = (x + dx) % SIDE
            for j in range(MOST):
                y_out[g, dx - 1, j] = pool[g, table[OUT + to * MOST + j]]
            y_copy(g, dx).start()

    def settle(g):
        for dx in range(SIDE):
            origin = (x + SIDE - dx) % SIDE
            at = pl.ds(pl.multiple_of((g * SIDE + origin) * rows, rows), rows)
            if dx:
                y_copy(g, dx).wait_recv()
            for j in range(MOST):
                if dx:
                    piece = y_in[g, dx - 1, j]
                else:
                    piece = pool[g, table[OUT + x * MOST + j]]
                k_ref[SLOTS + j, at, :] = piece[0]
                v_ref[SLOTS + j, at, :] = piece[1]

    def step(t, carry):
        early = t - nearest

        @pl.when((early >= 0) & (early < units))
        def _():
            g, c = split(early)

            @pl.when(c == 0)
            def _():
                x_arrive(g)

        k = t - z * SKEW

        @pl.when((k >= 0) & (k < units))
        def _():
            g, c = split(k)

            @pl.when(z > 0)
            def _():
                up_copy(k).wait_recv()
                pool[g, ITEMS + c] = up_in[k]

            @pl.when(z < SIDE - 1)
            def _():
                up_out[k] = pool[g, table[UP + c]]
                up_copy(k).start()

        m = t - (SIDE - 1 - z) * SKEW

        @pl.when((m >= 0) & (m < units))
        def _():
            g, c = split(m)

            @pl.when(z < SIDE - 1)
            def _():
                down_copy(m).wait_recv()
                pool[g, ITEMS + cap + c] = down_in[m]

            @pl.when(z > 0)
            def _():
                down_out[m] = pool[g, table[DOWN + c]]
                down_copy(m).start()

        late = t - farthest

        @pl.when(late >= 0)
        def _():
            g, c = split(late)

            @pl.when((c == 0) & (g < groups))
            def _():
                y_start(g)

            @pl.when((g >= 1) & (g <= groups))
            def _():
                @pl.when(c == 0)
                def _():
                    settle(g - 1)

                for slot in range(SLOTS):

                    @pl.when(c == slot + 1)
                    def _():
                        attend(g - 1, slot)

        return carry

    lax.fori_loop(0, units + (SIDE - 1) * SKEW + cap + SLOTS, step, 0)

    lane = lax.broadcasted_iota(jnp.int32, top.shape[1:], 1)
    for r in range(2):
        slot = (1 - half) * 2 + r
        p_out[r, 0] = acc[slot]
        p_out[r, 1] = jnp.where(lane < 64, top[slot], tot[slot])
    p_copy = pltpu.make_async_remote_copy(
        p_out, p_in, p_sem.at[0], p_sem.at[1], device_id=peer, device_id_type=MESH
    )
    p_copy.start()

    def x_drain(g, carry):
        for dx in range(1, SIDE):
            x_copy(g, dx).wait_send()
            y_copy(g, dx).wait_send()
        return carry

    lax.fori_loop(0, groups, x_drain, 0)

    def z_drain(k, carry):
        @pl.when(z < SIDE - 1)
        def _():
            up_copy(k).wait_send()

        @pl.when(z > 0)
        def _():
            down_copy(k).wait_send()

        return carry

    lax.fori_loop(0, units, z_drain, 0)
    w_copy.wait()
    p_copy.wait_recv()
    token = lax.broadcasted_iota(jnp.int32, (q_ref.shape[1], 1), 0) // size
    fresh_keys = [fk_ref[m].astype(jnp.float32) for m in range(news)]
    fresh_values = [fv_ref[m].astype(jnp.float32) for m in range(news)]
    for r in range(2):
        slot = half * 2 + r
        top_a, tot_a = top[slot][:, :1], tot[slot][:, :1]
        top_b, tot_b = p_in[r, 1][:, :1], p_in[r, 1][:, 64:65]
        asking = q_ref[r].astype(jnp.float32)
        peak = jnp.maximum(top_a, top_b)
        fresh = []
        for m in range(news):
            score = jnp.sum(asking * fresh_keys[m][r : r + 1], axis=1, keepdims=True) * scaling
            score = jnp.where(token >= m, score, LOW)
            fresh.append(score)
            peak = jnp.maximum(peak, score)
        scale_a = jnp.exp(top_a - peak)
        scale_b = jnp.exp(top_b - peak)
        summed = acc[slot] * scale_a + p_in[r, 0] * scale_b
        total = tot_a * scale_a + tot_b * scale_b
        for m in range(news):
            weight = jnp.where(token >= m, jnp.exp(fresh[m] - peak), 0.0)
            total = total + weight
            summed = summed + weight * fresh_values[m][r : r + 1]
        head[r] = summed / total
    for r in range(2):
        for a in range(size):
            for n in range(news):
                lhs[n * 2 + r : n * 2 + r + 1, a * 128 : (a + 1) * 128] = head[
                    r, n * size + a : n * size + a + 1, :
                ]
    left = lhs[...].astype(jnp.bfloat16)

    def s_copy(dt):
        return pltpu.make_async_remote_copy(
            s_out.at[dt],
            s_in.at[dt],
            s_send.at[dt],
            s_recv.at[dt],
            device_id=(inst, (tp + dt) % tps),
            device_id_type=MESH,
        )

    for dt in (6, 5, 7, 4, 2, 1, 3, 0):
        to = (tp + dt) % tps
        part = jnp.dot(
            left,
            w_buf[:, pl.ds(pl.multiple_of(to * cols, cols), cols)],
            preferred_element_type=jnp.float32,
        )
        if dt:
            s_out[dt] = jnp.concatenate([part[:, :wide], part[:, wide:]], axis=0).astype(jnp.bfloat16)
            s_copy(dt).start()
    mixed = part
    for dt in (1, 3, 2, 4, 5, 7, 6):
        s_copy(dt).wait_recv()
        folded = s_in[dt].astype(jnp.float32)
        mixed = mixed + jnp.concatenate([folded[:8], folded[8:]], axis=1)
    mix_ref[...] = mixed.astype(jnp.bfloat16)

    q_done = [p_copy]
    for copy in q_done:
        copy.wait_send()
    for dt in range(1, tps):
        s_copy(dt).wait_send()


def main_call(cap, collective_id, table, asking, fresh_key, fresh_value, keys, values, weight):
    slots, ctx, dim = keys.shape
    rows = ctx // (GROUPS * SIDE)
    tps = lax.axis_size("tp")
    cols = weight.shape[1] // tps
    news, own, width = asking.shape
    queries = news * (width // dim)
    unit = (2, rows, dim)
    units = GROUPS * cap
    bf16, f32 = jnp.bfloat16, jnp.float32
    vmem = pl.BlockSpec(memory_space=pltpu.VMEM)
    spread = pltpu.VMEM((GROUPS, SIDE - 1, MOST) + unit, bf16)
    line = pltpu.VMEM((units,) + unit, bf16)
    dma = pltpu.SemaphoreType.DMA
    return pl.pallas_call(
        functools.partial(main_kernel, cap),
        out_shape=(
            jax.ShapeDtypeStruct(keys.shape, bf16),
            jax.ShapeDtypeStruct(values.shape, bf16),
            jax.ShapeDtypeStruct((news * own, cols), bf16),
        ),
        in_specs=[
            pl.BlockSpec(memory_space=pltpu.SMEM),
            vmem,
            vmem,
            vmem,
            pl.BlockSpec(memory_space=pl.ANY),
            pl.BlockSpec(memory_space=pl.ANY),
            pl.BlockSpec(memory_space=pl.ANY),
        ],
        out_specs=(vmem, vmem, vmem),
        scratch_shapes=[
            pltpu.VMEM(weight.shape, bf16),
            pltpu.VMEM((slots + MOST, ctx, dim), bf16),
            pltpu.VMEM((slots + MOST, ctx, dim), bf16),
            pltpu.VMEM((own, queries, dim), f32),
            pltpu.VMEM((own, queries, dim), bf16),
            pltpu.VMEM((own, queries, dim), bf16),
            spread,
            spread,
            pltpu.VMEM((GROUPS, ITEMS + 2 * cap) + unit, bf16),
            line,
            line,
            line,
            line,
            spread,
            spread,
            pltpu.VMEM((slots, queries, dim), f32),
            pltpu.VMEM((slots, queries, dim), f32),
            pltpu.VMEM((slots, queries, dim), f32),
            pltpu.VMEM((2, 2, queries, dim), f32),
            pltpu.VMEM((2, 2, queries, dim), f32),
            pltpu.VMEM((2, queries, dim), f32),
            pltpu.VMEM((8, weight.shape[0]), f32),
            pltpu.VMEM((tps, 16, cols // 2), bf16),
            pltpu.VMEM((tps, 16, cols // 2), bf16),
            dma,
            dma((2,)),
            dma((2,)),
            dma((GROUPS, SIDE - 1)),
            dma((GROUPS, SIDE - 1)),
            dma((units,)),
            dma((units,)),
            dma((units,)),
            dma((units,)),
            dma((GROUPS, SIDE - 1)),
            dma((GROUPS, SIDE - 1)),
            dma((2,)),
            dma((tps,)),
            dma((tps,)),
        ],
        compiler_params=pltpu.CompilerParams(
            collective_id=collective_id, has_side_effects=True, vmem_limit_bytes=56 << 20
        ),
        name=f"move_attend_{cap}",
    )(table, asking, fresh_key, fresh_value, keys, values, weight)


def on_device(
    keys_cache,
    values_cache,
    queries,
    fresh_keys,
    fresh_values,
    out_weight,
    partner,
    chosen,
    lengths,
    dest_slot,
):
    _, slots, ctx, _, dim = keys_cache.shape
    news, own = queries.shape[:2]
    smem = pl.BlockSpec(memory_space=pltpu.SMEM)
    table = pl.pallas_call(
        plan_kernel,
        out_shape=jax.ShapeDtypeStruct((TABLE,), jnp.int32),
        in_specs=[smem] * 4,
        out_specs=smem,
        scratch_shapes=[pltpu.SMEM((16,), jnp.int32), pltpu.SMEM((16,), jnp.int32)],
        name="plan",
    )(partner, chosen.T, lengths.T, dest_slot.T)
    keys = keys_cache.reshape(slots, ctx, dim)
    values = values_cache.reshape(slots, ctx, dim)
    args = (table, queries, fresh_keys, fresh_values, keys, values, out_weight)
    if len(CAPS) == 1:
        moved_keys, moved_values, mixed = main_call(CAPS[0], 0, *args)
    else:
        moved_keys, moved_values, mixed = lax.switch(
            table[WHICH],
            [functools.partial(main_call, cap, i) for i, cap in enumerate(CAPS)],
            *args,
        )
    return (
        moved_keys.reshape(keys_cache.shape),
        moved_values.reshape(values_cache.shape),
        mixed.reshape(news, own, mixed.shape[1]),
    )


def solution(mesh):
    in_specs = (
        P("inst", None, None, "tp", None),
        P("inst", None, None, "tp", None),
        P(None, "inst", "tp"),
        P(None, "inst", "tp"),
        P(None, "inst", "tp"),
        P("tp", None),
        P(),
        P(),
        P(),
        P(),
    )
    out_specs = (
        P("inst", None, None, "tp", None),
        P("inst", None, None, "tp", None),
        P(None, "inst", "tp"),
    )
    return jax.shard_map(
        on_device, mesh=mesh, in_specs=in_specs, out_specs=out_specs, check_vma=False
    )
```

```python
import functools

import jax
import jax.numpy as jnp
from jax import lax
from jax.experimental import pallas as pl
from jax.experimental.pallas import tpu as pltpu
from jax.sharding import PartitionSpec as P

MESH = pl.DeviceIdType.MESH
LOW = -1e30
SLOTS = 4
MOST = 2
SIDE = 4
ITEMS = SIDE * MOST
WIDEST = ITEMS * 2
CAPS = (5, 6, 7, 8, 9, 10, 16)
GROUPS = 4
SKEW = 6
ATTEND = 2
FIRST = 1
LATER = 12
PAIR = 8
ASKING = 5
FAR, NEAR = (6, 5, 7, 4), (2, 1, 3)
UP, DOWN, OUT, SEL, SPAN, PICK, NONE, ASK, ASKED, TABLE = 0, 16, 32, 40, 44, 48, 50, 52, 54, 56


def where_am_i():
    inst = lax.axis_index("inst")
    chip = inst // 2
    return inst % 2, chip, chip // SIDE, chip % SIDE


def plan_kernel(partner, chosen, lengths, dest, table, variant, count, start):
    _, me, _, z = where_am_i()
    sent = []
    for i in range(16):
        count[i] = 0
    for s in range(16):
        sent.append(sum(chosen[r, s] for r in range(SLOTS)))
        cls = (s % SIDE) * SIDE + partner[s] % SIDE
        count[cls] = count[cls] + sent[s]
    n = [[count[a * SIDE + b] for b in range(SIDE)] for a in range(SIDE)]

    def flip(a, b, down):
        return n[3 - a][3 - b] if down else n[a][b]

    need = 0
    for down in (False, True):
        f = functools.partial(flip, down=down)
        need = functools.reduce(
            jnp.maximum,
            (
                need,
                f(0, 1) + f(0, 2) + f(0, 3),
                f(0, 2) + f(0, 3) + f(1, 2) + f(1, 3),
                f(0, 3) + f(1, 3) + f(2, 3),
            ),
        )
    which, cap = 0, CAPS[0]
    for i in range(1, len(CAPS)):
        which = jnp.where(need > CAPS[i - 1], i, which)
        cap = jnp.where(need > CAPS[i - 1], CAPS[i], cap)
    variant[0] = which
    for down in (False, True):
        f = functools.partial(flip, down=down)
        places = {
            (0, 3): 0,
            (1, 3): f(0, 3),
            (1, 2): f(0, 3) + f(1, 3),
            (0, 2): cap - f(0, 2),
            (0, 1): f(0, 3),
            (2, 3): f(0, 3) + f(1, 3),
        }
        for (a, b), place in places.items():
            start[(3 - a) * SIDE + 3 - b if down else a * SIDE + b] = place
    for a in range(SIDE):
        start[a * SIDE + a] = 0
    for c in range(WIDEST):
        table[UP + c] = jnp.where(z == 0, 0, ITEMS + c)
        table[DOWN + c] = jnp.where(z == SIDE - 1, 0, ITEMS + cap + c)
    for i in range(OUT, TABLE):
        table[i] = 0
    source = 0
    for s in range(16):
        d = partner[s]
        source = jnp.where(d == me, s, source)
        zs, xs = s % SIDE, s // SIDE
        zd, xd = d % SIDE, d // SIDE
        base = start[zs * SIDE + zd]
        start[zs * SIDE + zd] = base + sent[s]
        for j in range(MOST):
            valid = j < sent[s]
            leaves = valid & (zs == z) & (zd != zs)
            place = jnp.where(zd > zs, UP, DOWN) + base + j
            table[jnp.where(leaves, place, NONE)] = xs * MOST + j
            lands = valid & (zd == z)
            kept = jnp.where(zs < z, ITEMS + base + j, ITEMS + cap + base + j)
            kept = jnp.where(zs == z, xs * MOST + j, kept)
            table[jnp.where(lands, OUT + xd * MOST + j, NONE)] = kept
    mine, theirs = 0, 0
    for r in range(SLOTS):
        table[SEL + r] = r
        table[SPAN + r] = lengths[r, me]
    for r in range(SLOTS):
        go = chosen[r, me] == 1
        table[jnp.where(go, PICK + mine, NONE)] = r
        table[jnp.where(go, ASK + mine, NONE)] = partner[me] * 2 + dest[r, me] % 2
        table[jnp.where(go, ASKED + mine, NONE)] = dest[r, me] // 2
        mine = mine + jnp.where(go, 1, 0)
        come = chosen[r, source] == 1
        slot = dest[r, source]
        theirs = theirs + jnp.where(come, 1, 0)
        table[jnp.where(come, SEL + slot, NONE)] = SLOTS - 1 + theirs


def main_kernel(cap, table, *refs):
    (raw_ref, fk_ref, fv_ref, k_hbm, v_hbm, w_hbm, mk_ref, mv_ref, mix_ref, *refs) = refs
    (w_buf, k_ref, v_ref, q_rows, q_ref, q_peer, *refs) = refs
    (z_in, line_q, x_in_q, all_q, pick_q, peer_q, slot_q, part, gone, *refs) = refs
    (x_out, x_in, pool, up_out, up_in, down_out, down_in, y_out, y_in, *refs) = refs
    (px_out, px_in, p_pool, p_up_out, p_up_in, p_down_out, p_down_in, py_out, py_in, *refs) = refs
    (p_out, p_in, head, lhs, s_out, s_in, *refs) = refs
    (w_sem, kv_sem, q_sem, zq_sem, xq_sem, cq_sem, p_sem, s_sem, *refs) = refs
    (x_sem, up_sem, down_sem, y_sem, px_sem, p_up_sem, p_down_sem, py_sem) = refs
    groups = x_out.shape[0]
    rows = x_out.shape[4]
    thin = px_out.shape[3]
    ctx = k_ref.shape[1]
    span = ctx // groups
    tps = s_out.shape[0]
    cols = mix_ref.shape[1]
    wide = cols // 2
    news, _, width = raw_ref.shape
    dim = k_ref.shape[2]
    size = width // dim
    queries = news * size
    blocks = groups + 1
    special = groups // 2
    units = blocks * cap
    scaling = dim**-0.5
    half, chip, x, z = where_am_i()
    inst = lax.axis_index("inst")
    tp = lax.axis_index("tp")
    peer = (inst + 1 - 2 * half, tp)

    def along_x(dx):
        return (((x + dx) % SIDE * SIDE + z) * 2 + half, tp)

    def along_z(dz):
        return ((x * SIDE + (z + dz) % SIDE) * 2 + half, tp)

    above = (inst + 2, tp)
    below = (inst - 2, tp)

    def remote(source, target, sems, device):
        return pltpu.make_async_remote_copy(
            source, target, sems[0], sems[1], device_id=device, device_id_type=MESH
        )

    k_copy = pltpu.make_async_copy(k_hbm, k_ref.at[:SLOTS], kv_sem.at[0])
    v_copy = pltpu.make_async_copy(v_hbm, v_ref.at[:SLOTS], kv_sem.at[1])
    k_copy.start()
    v_copy.start()
    barrier = pltpu.get_barrier_semaphore()

    def greet(device):
        pl.semaphore_signal(barrier, inc=1, device_id=device, device_id_type=MESH)

    greet(peer)
    for d in range(1, SIDE):
        greet(along_x(d))
        greet(along_z(d))
    for dt in range(1, tps):
        greet((inst, (tp + dt) % tps))
    w_copy = pltpu.make_async_copy(w_hbm, w_buf, w_sem)

    for n in range(news):
        raw = raw_ref[n].astype(jnp.float32)
        for r in range(2):
            for a in range(size):
                q_rows[r, n * size + a : n * size + a + 1, :] = raw[
                    r : r + 1, a * dim : (a + 1) * dim
                ]
    for r in range(2):
        q_ref[r] = q_rows[r].astype(jnp.bfloat16)
    k_copy.wait()
    v_copy.wait()

    def stage(g):
        for dx in range(SIDE):
            to = (x + dx) % SIDE
            at = pl.ds(pl.multiple_of((g * SIDE + to) * rows, rows), rows)
            for j in range(MOST):
                slot = table[PICK + j]
                for kv, ref in enumerate((k_ref, v_ref)):
                    piece = ref[slot, at, :]
                    if dx == 0:
                        pool[g, x * MOST + j, kv] = piece
                    else:
                        x_out[g, dx - 1, j, kv] = piece

    def x_copy(g, dx):
        i = dx - 1
        sems = (x_sem.at[0, g, i], x_sem.at[1, g, i])
        return remote(x_out.at[g, i], x_in.at[g, i], sems, along_x(dx))

    def y_copy(g, dx):
        i = dx - 1
        sems = (y_sem.at[0, g, i], y_sem.at[1, g, i])
        return remote(y_out.at[g, i], y_in.at[g, i], sems, along_x(dx))

    def px_copy(dx):
        i = dx - 1
        return remote(
            px_out.at[i], px_in.at[i], (px_sem.at[0, i], px_sem.at[1, i]), along_x(dx)
        )

    def py_copy(dx):
        i = dx - 1
        return remote(
            py_out.at[i], py_in.at[i], (py_sem.at[0, i], py_sem.at[1, i]), along_x(dx)
        )

    def up_copy(k):
        return remote(up_out.at[k], up_in.at[k], (up_sem.at[0, k], up_sem.at[1, k]), above)

    def down_copy(k):
        return remote(
            down_out.at[k], down_in.at[k], (down_sem.at[0, k], down_sem.at[1, k]), below
        )

    def p_up_copy(c):
        sems = (p_up_sem.at[0, c], p_up_sem.at[1, c])
        return remote(p_up_out.at[c], p_up_in.at[c], sems, above)

    def p_down_copy(c):
        sems = (p_down_sem.at[0, c], p_down_sem.at[1, c])
        return remote(p_down_out.at[c], p_down_in.at[c], sems, below)

    def zq_copy(dz):
        i = dz - 1
        return remote(q_ref, z_in.at[i], (zq_sem.at[0, i], zq_sem.at[1, i]), along_z(dz))

    def xq_copy(dx):
        i = dx - 1
        return remote(line_q, x_in_q.at[i], (xq_sem.at[0, i], xq_sem.at[1, i]), along_x(dx))

    q_copy = remote(q_ref, q_peer, (q_sem.at[0], q_sem.at[1]), peer)
    cq_copy = remote(pick_q, peer_q, (cq_sem.at[0], cq_sem.at[1]), peer)
    p_copy = remote(p_out, p_in, (p_sem.at[0], p_sem.at[1]), peer)

    def s_copy(dt):
        sems = (s_sem.at[0, dt], s_sem.at[1, dt])
        return remote(s_out.at[dt], s_in.at[dt], sems, (inst, (tp + dt) % tps))

    def x_start(g):
        for dx in (1, 3, 2):
            x_copy(g, dx).start()

    stage(0)
    pl.semaphore_wait(barrier, 1 + 2 * (SIDE - 1) + tps - 1)
    x_start(0)
    for dz in range(1, SIDE):
        zq_copy(dz).start()
    q_copy.start()

    def stage_rest(g, carry):
        stage(g)
        return carry

    lax.fori_loop(1, groups, stage_rest, 0)

    nearest = jnp.minimum(z, SIDE - 1 - z) * SKEW
    farthest = jnp.maximum(z, SIDE - 1 - z) * SKEW + cap - 1

    factor = -(-(1 << 16) // cap)

    def split(k):
        b = lax.shift_right_arithmetic(k * factor, 16)
        return b, k - b * cap

    def group_of(b):
        return jnp.where(b > special, b - 1, b)

    def spread_queries():
        line_q[z] = q_ref[...]
        for dz in range(1, SIDE):
            zq_copy(dz).wait_recv()
            line_q[(z + SIDE - dz) % SIDE] = z_in[dz - 1]
        for dx in (1, 3, 2):
            xq_copy(dx).start()
        for i in range(SIDE):
            for r in range(2):
                all_q[(x * SIDE + i) * 2 + r] = line_q[i, r]

    def pick_queries():
        for dx in range(1, SIDE):
            xq_copy(dx).wait_recv()
            origin = (x + SIDE - dx) % SIDE
            for i in range(SIDE):
                for r in range(2):
                    all_q[(origin * SIDE + i) * 2 + r] = x_in_q[dx - 1, i, r]
        for j in range(MOST):
            pick_q[j] = all_q[table[ASK + j]]
        cq_copy.start()

    def own_queries():
        q_copy.wait_recv()
        for r in range(2):
            slot_q[half * 2 + r] = q_ref[r]
            slot_q[(1 - half) * 2 + r] = q_peer[r]

    def far_queries():
        cq_copy.wait_recv()
        for j in range(MOST):
            here = table[ASKED + j] == half
            slot_q[SLOTS + j] = jnp.where(here, pick_q[j], peer_q[j])

    lane = lax.broadcasted_iota(jnp.int32, (queries, dim), 1)

    def attend(asking, slot, out):
        scores = (
            lax.dot_general(
                asking,
                k_ref[slot],
                (((1,), (1,)), ((), ())),
                preferred_element_type=jnp.float32,
            )
            * scaling
        )
        spot = half * ctx + lax.broadcasted_iota(jnp.int32, (queries, ctx), 1)
        usable = spot < table[SPAN + slot]
        highest = jnp.max(jnp.where(usable, scores, LOW), axis=1, keepdims=True)
        weights = jnp.where(usable, jnp.exp(scores - highest), 0.0)
        total = jnp.sum(weights, axis=1, keepdims=True)
        out[0] = jnp.dot(
            weights.astype(jnp.bfloat16), v_ref[slot], preferred_element_type=jnp.float32
        )
        out[1] = jnp.where(lane < 64, highest, total)

    def px_start():
        for dx in range(SIDE):
            to = (x + dx) % SIDE
            at = pl.ds(pl.multiple_of(to * thin, thin), thin)
            for j in range(MOST):
                for kv in range(2):
                    piece = gone[j, kv, at, :]
                    if dx == 0:
                        p_pool[x * MOST + j, kv] = piece
                    else:
                        px_out[dx - 1, j, kv] = piece
        for dx in (1, 3, 2):
            px_copy(dx).start()

    def x_arrive(g):
        for dx in range(1, SIDE):
            x_copy(g, dx).wait_recv()
            origin = (x + SIDE - dx) % SIDE
            for j in range(MOST):
                pool[g, origin * MOST + j] = x_in[g, dx - 1, j]

    def px_arrive():
        for dx in range(1, SIDE):
            px_copy(dx).wait_recv()
            origin = (x + SIDE - dx) % SIDE
            for j in range(MOST):
                p_pool[origin * MOST + j] = px_in[dx - 1, j]

    def y_start(g):
        for dx in (1, 3, 2):
            to = (x + dx) % SIDE
            for j in range(MOST):
                y_out[g, dx - 1, j] = pool[g, table[OUT + to * MOST + j]]
            y_copy(g, dx).start()

    def py_start():
        for dx in (1, 3, 2):
            to = (x + dx) % SIDE
            for j in range(MOST):
                py_out[dx - 1, j] = p_pool[table[OUT + to * MOST + j]]
            py_copy(dx).start()

    def settle(g):
        for dx in range(SIDE):
            origin = (x + SIDE - dx) % SIDE
            at = pl.ds(pl.multiple_of((g * SIDE + origin) * rows, rows), rows)
            if dx:
                y_copy(g, dx).wait_recv()
            for j in range(MOST):
                if dx:
                    piece = y_in[g, dx - 1, j]
                else:
                    piece = pool[g, table[OUT + x * MOST + j]]
                k_ref[SLOTS + j, at, :] = piece[0]
                v_ref[SLOTS + j, at, :] = piece[1]

    def emit(g):
        at = pl.ds(pl.multiple_of(g * span, span), span)
        for slot in range(SLOTS):
            source = table[SEL + slot]
            mk_ref[slot, at, :] = k_ref[source, at, :]
            mv_ref[slot, at, :] = v_ref[source, at, :]

    def p_settle():
        for dx in range(SIDE):
            origin = (x + SIDE - dx) % SIDE
            at = pl.ds(pl.multiple_of(origin * thin, thin), thin)
            if dx:
                py_copy(dx).wait_recv()
            for j in range(MOST):
                if dx:
                    piece = py_in[dx - 1, j]
                else:
                    piece = p_pool[table[OUT + x * MOST + j]]
                part[SLOTS + j, 0, at, :] = piece[0]
                part[SLOTS + j, 1, at, :] = piece[1]
        for r in range(2):
            p_out[r] = part[table[SEL + (1 - half) * 2 + r]]
        p_copy.start()

    def combine():
        p_copy.wait_recv()
        token = lax.broadcasted_iota(jnp.int32, (queries, 1), 0) // size
        fresh_keys = [fk_ref[m].astype(jnp.float32) for m in range(news)]
        fresh_values = [fv_ref[m].astype(jnp.float32) for m in range(news)]
        for r in range(2):
            mine = part[table[SEL + half * 2 + r]]
            top_a, tot_a = mine[1][:, :1], mine[1][:, 64:65]
            top_b, tot_b = p_in[r, 1][:, :1], p_in[r, 1][:, 64:65]
            asking = q_rows[r]
            peak = jnp.maximum(top_a, top_b)
            fresh = []
            for m in range(news):
                score = jnp.sum(asking * fresh_keys[m][r : r + 1], axis=1, keepdims=True)
                score = jnp.where(token >= m, score * scaling, LOW)
                fresh.append(score)
                peak = jnp.maximum(peak, score)
            scale_a = jnp.exp(top_a - peak)
            scale_b = jnp.exp(top_b - peak)
            summed = mine[0] * scale_a + p_in[r, 0] * scale_b
            total = tot_a * scale_a + tot_b * scale_b
            for m in range(news):
                weight = jnp.where(token >= m, jnp.exp(fresh[m] - peak), 0.0)
                total = total + weight
                summed = summed + weight * fresh_values[m][r : r + 1]
            head[r] = summed / total
        for r in range(2):
            for a in range(size):
                for n in range(news):
                    lhs[n * 2 + r : n * 2 + r + 1, a * dim : (a + 1) * dim] = head[
                        r, n * size + a : n * size + a + 1, :
                    ]
        w_copy.wait()

    def project(dt):
        to = (tp + dt) % tps
        part_out = jnp.dot(
            lhs[...].astype(jnp.bfloat16),
            w_buf[:, pl.ds(pl.multiple_of(to * cols, cols), cols)],
            preferred_element_type=jnp.float32,
        )
        if dt == 0:
            return part_out
        folded = jnp.concatenate([part_out[:, :wide], part_out[:, wide:]], axis=0)
        s_out[dt] = folded.astype(jnp.bfloat16)
        s_copy(dt).start()

    spread_queries()
    for g in range(1, 1 + FIRST):
        x_start(g)
    w_copy.start()

    settled = [(g, (g if g < special else g + 1) * cap + LATER) for g in range(groups - 1)]

    pair_at = min(special * cap + PAIR, groups * cap - 2)

    def step(t, carry):
        early = t - nearest

        @pl.when((early >= 0) & (early < units))
        def _():
            b, c = split(early)

            @pl.when((c == 0) & (b != special))
            def _():
                x_arrive(group_of(b))

            @pl.when(early == special * cap)
            def _():
                px_arrive()

            for g in range(1 + FIRST, groups):

                @pl.when(early == 5 + (g - 1 - FIRST) * cap)
                def _():
                    x_start(g)

            @pl.when(early == ASKING)
            def _():
                pick_queries()

            @pl.when(early == ASKING + 2)
            def _():
                far_queries()

            for j in range(MOST):

                @pl.when(early == ASKING + 2 + j)
                def _():
                    attend(slot_q[SLOTS + j], table[PICK + j], gone.at[j])

            @pl.when(early == ASKING + 2 + MOST)
            def _():
                px_start()

            @pl.when(early == ASKING + 3 + MOST)
            def _():
                own_queries()

            for slot in range(SLOTS):

                @pl.when(early == ASKING + 3 + MOST + slot * ATTEND)
                def _():
                    attend(slot_q[slot], slot, part.at[slot])

        k = t - z * SKEW

        @pl.when((k >= 0) & (k < units))
        def _():
            b, c = split(k)

            @pl.when(b != special)
            def _():
                g = group_of(b)
                i = g * cap + c

                @pl.when(z > 0)
                def _():
                    up_copy(i).wait_recv()
                    pool[g, ITEMS + c] = up_in[i]

                @pl.when(z < SIDE - 1)
                def _():
                    up_out[i] = pool[g, table[UP + c]]
                    up_copy(i).start()

            @pl.when(b == special)
            def _():
                @pl.when(z > 0)
                def _():
                    p_up_copy(c).wait_recv()
                    p_pool[ITEMS + c] = p_up_in[c]

                @pl.when(z < SIDE - 1)
                def _():
                    p_up_out[c] = p_pool[table[UP + c]]
                    p_up_copy(c).start()

        m = t - (SIDE - 1 - z) * SKEW

        @pl.when((m >= 0) & (m < units))
        def _():
            b, c = split(m)

            @pl.when(b != special)
            def _():
                g = group_of(b)
                i = g * cap + c

                @pl.when(z < SIDE - 1)
                def _():
                    down_copy(i).wait_recv()
                    pool[g, ITEMS + cap + c] = down_in[i]

                @pl.when(z > 0)
                def _():
                    down_out[i] = pool[g, table[DOWN + c]]
                    down_copy(i).start()

            @pl.when(b == special)
            def _():
                @pl.when(z < SIDE - 1)
                def _():
                    p_down_copy(c).wait_recv()
                    p_pool[ITEMS + cap + c] = p_down_in[c]

                @pl.when(z > 0)
                def _():
                    p_down_out[c] = p_pool[table[DOWN + c]]
                    p_down_copy(c).start()

        late = t - farthest

        @pl.when(late >= 0)
        def _():
            b, c = split(late)

            @pl.when((c == 0) & (b != special) & (b < blocks))
            def _():
                y_start(group_of(b))

            @pl.when(late == special * cap)
            def _():
                py_start()

            @pl.when(late == pair_at)
            def _():
                p_settle()

            @pl.when(late == pair_at + 2)
            def _():
                combine()

            for g, at in settled:
                if at <= groups * cap:

                    @pl.when(late == at)
                    def _():
                        settle(g)

                    @pl.when(late == at)
                    def _():
                        emit(g)

        return carry

    lax.fori_loop(0, units + (SIDE - 1) * SKEW, step, 0)

    for dt in FAR + NEAR:
        project(dt)
    mixed = project(0)
    for g, at in settled:
        if at > groups * cap:
            settle(g)
            emit(g)
    settle(groups - 1)
    emit(groups - 1)

    def x_drain(g, carry):
        for dx in range(1, SIDE):
            x_copy(g, dx).wait_send()
            y_copy(g, dx).wait_send()
        return carry

    lax.fori_loop(0, groups, x_drain, 0)
    for d in range(1, SIDE):
        px_copy(d).wait_send()
        py_copy(d).wait_send()
        zq_copy(d).wait_send()
        xq_copy(d).wait_send()
    q_copy.wait_send()
    cq_copy.wait_send()
    p_copy.wait_send()

    @pl.when(z < SIDE - 1)
    def _():
        def drain(k, carry):
            up_copy(k).wait_send()
            return carry

        def p_drain(k, carry):
            p_up_copy(k).wait_send()
            return carry

        lax.fori_loop(0, groups * cap, drain, 0)
        lax.fori_loop(0, cap, p_drain, 0)

    @pl.when(z > 0)
    def _():
        def drain(k, carry):
            down_copy(k).wait_send()
            return carry

        def p_drain(k, carry):
            p_down_copy(k).wait_send()
            return carry

        lax.fori_loop(0, groups * cap, drain, 0)
        lax.fori_loop(0, cap, p_drain, 0)

    for dt in NEAR + FAR:
        s_copy(dt).wait_recv()
        folded = s_in[dt].astype(jnp.float32)
        mixed = mixed + jnp.concatenate([folded[:8], folded[8:]], axis=1)
        s_copy(dt).wait_send()
    mix_ref[...] = mixed.astype(jnp.bfloat16)


def main_call(cap, collective_id, table, asking, fresh_key, fresh_value, keys, values, weight):
    slots, ctx, dim = keys.shape
    rows = ctx // (GROUPS * SIDE)
    tps = lax.axis_size("tp")
    cols = weight.shape[1] // tps
    news, own, width = asking.shape
    queries = news * (width // dim)
    unit = (2, rows, dim)
    thin = (2, queries // SIDE, dim)
    bf16, f32 = jnp.bfloat16, jnp.float32
    vmem = pl.BlockSpec(memory_space=pltpu.VMEM)
    hbm = pl.BlockSpec(memory_space=pl.ANY)
    dma = pltpu.SemaphoreType.DMA
    cache = pltpu.VMEM((slots + MOST, ctx, dim), bf16)
    asked = pltpu.VMEM((own, queries, dim), bf16)
    spread = pltpu.VMEM((GROUPS, SIDE - 1, MOST) + unit, bf16)
    line = pltpu.VMEM((GROUPS * cap,) + unit, bf16)
    thin_spread = pltpu.VMEM((SIDE - 1, MOST) + thin, f32)
    thin_line = pltpu.VMEM((cap,) + thin, f32)
    pair = pltpu.VMEM((2, 2, queries, dim), f32)
    sums = pltpu.VMEM((tps, 2 * news * own, cols // 2), bf16)
    return pl.pallas_call(
        functools.partial(main_kernel, cap),
        out_shape=(
            jax.ShapeDtypeStruct(keys.shape, bf16),
            jax.ShapeDtypeStruct(values.shape, bf16),
            jax.ShapeDtypeStruct((news * own, cols), bf16),
        ),
        in_specs=[pl.BlockSpec(memory_space=pltpu.SMEM), vmem, vmem, vmem, hbm, hbm, hbm],
        out_specs=(vmem, vmem, vmem),
        scratch_shapes=[
            pltpu.VMEM(weight.shape, bf16),
            cache,
            cache,
            pltpu.VMEM((own, queries, dim), f32),
            asked,
            asked,
            pltpu.VMEM((SIDE - 1, own, queries, dim), bf16),
            pltpu.VMEM((SIDE, own, queries, dim), bf16),
            pltpu.VMEM((SIDE - 1, SIDE, own, queries, dim), bf16),
            pltpu.VMEM((SIDE * SIDE * own, queries, dim), bf16),
            asked,
            asked,
            pltpu.VMEM((slots + MOST, queries, dim), bf16),
            pltpu.VMEM((slots + MOST, 2, queries, dim), f32),
            pair,
            spread,
            spread,
            pltpu.VMEM((GROUPS, ITEMS + 2 * cap) + unit, bf16),
            line,
            line,
            line,
            line,
            spread,
            spread,
            thin_spread,
            thin_spread,
            pltpu.VMEM((ITEMS + 2 * cap,) + thin, f32),
            thin_line,
            thin_line,
            thin_line,
            thin_line,
            thin_spread,
            thin_spread,
            pair,
            pair,
            pltpu.VMEM((own, queries, dim), f32),
            pltpu.VMEM((news * own, weight.shape[0]), f32),
            sums,
            sums,
            dma,
            dma((2,)),
            dma((2,)),
            dma((2, SIDE - 1)),
            dma((2, SIDE - 1)),
            dma((2,)),
            dma((2,)),
            dma((2, tps)),
            dma((2, GROUPS, SIDE - 1)),
            dma((2, GROUPS * cap)),
            dma((2, GROUPS * cap)),
            dma((2, GROUPS, SIDE - 1)),
            dma((2, SIDE - 1)),
            dma((2, cap)),
            dma((2, cap)),
            dma((2, SIDE - 1)),
        ],
        compiler_params=pltpu.CompilerParams(
            collective_id=collective_id, has_side_effects=True, vmem_limit_bytes=56 << 20
        ),
        name=f"move_attend_{cap}",
    )(table, asking, fresh_key, fresh_value, keys, values, weight)


def on_device(
    keys_cache,
    values_cache,
    queries,
    fresh_keys,
    fresh_values,
    out_weight,
    partner,
    chosen,
    lengths,
    dest_slot,
):
    _, slots, ctx, _, dim = keys_cache.shape
    news, own = queries.shape[:2]
    smem = pl.BlockSpec(memory_space=pltpu.SMEM)
    table, variant = pl.pallas_call(
        plan_kernel,
        out_shape=(
            jax.ShapeDtypeStruct((TABLE,), jnp.int32),
            jax.ShapeDtypeStruct((1,), jnp.int32),
        ),
        in_specs=[smem] * 4,
        out_specs=(smem, smem),
        scratch_shapes=[pltpu.SMEM((16,), jnp.int32), pltpu.SMEM((16,), jnp.int32)],
        name="plan",
    )(partner, chosen.T, lengths.T, dest_slot.T)
    keys = keys_cache.reshape(slots, ctx, dim)
    values = values_cache.reshape(slots, ctx, dim)
    args = (table, queries, fresh_keys, fresh_values, keys, values, out_weight)
    if len(CAPS) == 1:
        moved_keys, moved_values, mixed = main_call(CAPS[0], 0, *args)
    else:
        moved_keys, moved_values, mixed = lax.switch(
            variant[0],
            [functools.partial(main_call, cap, i) for i, cap in enumerate(CAPS)],
            *args,
        )
    return (
        moved_keys.reshape(keys_cache.shape),
        moved_values.reshape(values_cache.shape),
        mixed.reshape(news, own, mixed.shape[1]),
    )


def solution(mesh):
    in_specs = (
        P("inst", None, None, "tp", None),
        P("inst", None, None, "tp", None),
        P(None, "inst", "tp"),
        P(None, "inst", "tp"),
        P(None, "inst", "tp"),
        P("tp", None),
        P(),
        P(),
        P(),
        P(),
    )
    out_specs = (
        P("inst", None, None, "tp", None),
        P("inst", None, None, "tp", None),
        P(None, "inst", "tp"),
    )
    return jax.shard_map(
        on_device, mesh=mesh, in_specs=in_specs, out_specs=out_specs, check_vma=False
    )
```
